512 devices in a mesh: pts: 128 (over x, z, core), chan: 4 (over y).
Axes of the slice: x: 4, y: 4, z: 16, core: 2. Of those that a mesh axis runs over, the one named last changes fastest.
Arguments:
- feats: bfloat16 [131072, 512], P('pts', 'chan'), may hold values from -6 to 6
- dest_pos: int32 [131072], P('pts'), may hold values from 0 to 131071, as said below
- cell_id: int32 [131072], P('pts'), may hold values from 0 to 16383, as said below
- ln1_gain: float32 [512], replicated, may hold values from 0.1 to 1.9
- w_qkv: bfloat16 [3, 512, 512], P(None, None, 'chan')
- w_out: bfloat16 [512, 512], P('chan'), may hold values from -1 to 1
- ln2_gain: float32 [512], replicated, may hold values from 0.1 to 1.9
- w_fc1: bfloat16 [512, 2048], P(None, 'chan'), may hold values from -0.25 to 0.25
- w_fc2: bfloat16 [2048, 512], P('chan'), may hold values from -0.25 to 0.25
- w_pool: bfloat16 [512, 512], P(None, 'chan'), may hold values from -0.25 to 0.25
Outputs:
- block_out: bfloat16 [131072, 512], P('pts', 'chan')
- pooled: bfloat16 [16384, 512], P('pts', 'chan')
The draws below stay inside these ranges and needn't reach their ends.
Inputs may be any that keep to these rules, and one draw needn't show every extreme that they name: `dest_pos`: A permutation of the points. Device i of pts sends its points only to devices i - 3 to i + 3 and i + 128 / 2 (cyclic); every device sends the same number of points to the device at a given one of these eight offsets, 192 to one of them and fewer to the others. `cell_id`: never falls along the points; every cell has at least one point; the points of cells b * 128 to (b + 1) * 128 - 1 lie on devices b - 1, b and b + 1 of pts, on both neighbours for some b.
All inputs are finite; a program needn't handle non-finite values.
Results may differ from the reference program's by a relative error of at most 0.023.
The reference program's roundings to bfloat16 on the way (of `ordered`, `normed`, `qkv`, `probs`, `attn`, `mid`, `normed2` and `act`) count: a program that leaves them out, or rounds other values in their place, can miss the bound.
Values may be sent and summed in bfloat16 or wider, within the bound.
No kernel may reach another device: no remote copies, remote signals or barrier semaphores. Data moves between devices by JAX's collectives and lax.ppermute only.
A program may use at most 64 MiB of HBM per device.

```python
import jax
import jax.numpy as jnp
from jax import lax

C = 512
HEADS = 32
FF = 2048
PATCH = 1024
ROWS = 1024
NPTS = 131072
NCELL = 16384


def draw_dest_pos(key, part):
    key = jax.random.fold_in(key, 3)
    ndev = NPTS // ROWS
    unit = ROWS // 64
    key_counts, key_send, key_recv = jax.random.split(key, 3)
    base = jnp.array([12, 10, 9, 8, 8, 7, 6, 4], jnp.int32) * unit
    counts = base[jax.random.permutation(key_counts, 8)]
    ends = jnp.cumsum(counts)
    listing = jnp.arange(ROWS, dtype=jnp.int32)
    offset = jnp.sum((listing[:, None] >= ends[None, :]).astype(jnp.int32), axis=1)
    deltas = jnp.array([-3, -2, -1, 0, 1, 2, 3, ndev // 2], jnp.int32)
    send_order = jax.vmap(lambda k: jax.random.permutation(k, ROWS))(jax.random.split(key_send, ndev)).astype(jnp.int32)
    recv_order = jax.vmap(lambda k: jax.random.permutation(k, ROWS))(jax.random.split(key_recv, ndev)).astype(jnp.int32)
    devices = jnp.arange(ndev, dtype=jnp.int32)[:, None]
    target = (devices + deltas[offset][None, :]) % ndev
    dest_global = target * ROWS + recv_order[target, listing[None, :]]
    src_global = devices * ROWS + send_order
    return jnp.zeros((NPTS,), jnp.int32).at[src_global.reshape(-1)].set(dest_global.reshape(-1))


def draw_cell_id(key, part):
    key = jax.random.fold_in(key, 7)
    ndev = NPTS // ROWS
    cells = ROWS // 8
    reach = ROWS // 4
    width = ROWS + 2 * reach
    key_shift, key_cut = jax.random.split(key)
    shifts = jax.random.randint(key_shift, (ndev,), -reach, reach + 1).astype(jnp.int32)
    shifts = shifts.at[ndev - 1].set(0)
    ends = (jnp.arange(ndev, dtype=jnp.int32) + 1) * ROWS + shifts
    starts = jnp.concatenate([jnp.zeros((1,), jnp.int32), ends[:-1]])
    lengths = ends - starts
    scores = jax.vmap(lambda k: jax.random.permutation(k, width))(jax.random.split(key_cut, ndev)).astype(jnp.int32)
    places = jnp.arange(width, dtype=jnp.int32)
    valid = (places[None, :] >= 1) & (places[None, :] < lengths[:, None])
    scores = jnp.where(valid, scores, -1)
    picked = lax.top_k(scores, cells - 1)[1]
    marks = jnp.zeros((ndev, width), jnp.int32).at[jnp.arange(ndev)[:, None], picked].set(1)
    local_cell = jnp.cumsum(marks, axis=1)
    points = jnp.arange(NPTS, dtype=jnp.int32)
    block = jnp.searchsorted(ends, points, side='right').astype(jnp.int32)
    inside = points - starts[block]
    return (block * cells + local_cell[block, inside]).astype(jnp.int32)


def draw_w_qkv(key, part):
    key = jax.random.fold_in(key, 11)
    weights = jax.random.normal(key, (3, C, C), jnp.float32) * C ** (-0.5)
    return weights.astype(jnp.bfloat16)


def shard_levels(rng, extent, cuts, low, high):
    def one(dim, parts):
        steps = jax.random.uniform(jax.random.fold_in(jax.random.fold_in(rng, 6), dim), (parts,), jnp.float32, low / len(cuts), high / len(cuts))
        return jnp.repeat(jnp.exp(steps), extent[dim] // parts).reshape((-1,) + (1,) * (len(extent) - dim - 1))

    loudness = one(*cuts[0])
    for cut in cuts[1:]:
        loudness = loudness * one(*cut)
    return loudness


def scatter_about(own_key, extent, spread, limit, pieces=(), held_as=jnp.bfloat16):
    drawn = jax.random.normal(own_key, extent, jnp.float32) * spread
    if len(pieces) > 0:
        drawn = shard_levels(own_key, extent, pieces, -0.22, 0.18) * drawn
    return jnp.clip(drawn, min=-limit, max=limit).astype(held_as)


def setup_inputs(seed: int = 0) -> dict:
    streams_of = jax.random.split(jax.random.key(seed), 11)
    return {
        "feats": scatter_about(streams_of[0], (NPTS, C), 1.0, 6.0, ((0, 128), (1, 4))),
        "dest_pos": draw_dest_pos(jax.random.fold_in(streams_of[10], 71), 0),
        "cell_id": draw_cell_id(jax.random.fold_in(streams_of[10], 71), 0),
        "ln1_gain": jnp.clip(1.0 + 0.18 * jax.random.normal(streams_of[3], (C,), jnp.float32), 0.1, 1.9),
        "w_qkv": draw_w_qkv(jax.random.fold_in(streams_of[10], 71), 0),
        "w_out": scatter_about(streams_of[5], (C, C), (C // 16) ** -0.5, 1.0, ((0, 4),)),
        "ln2_gain": jnp.clip(1.0 + 0.18 * jax.random.normal(streams_of[6], (C,), jnp.float32), 0.1, 1.9),
        "w_fc1": scatter_about(streams_of[7], (C, FF), C ** -0.5, 0.25, ((1, 4),)),
        "w_fc2": scatter_about(streams_of[8], (FF, C), (FF // 4) ** -0.5, 0.25, ((0, 4),)),
        "w_pool": scatter_about(streams_of[9], (C, C), C ** -0.5, 0.25, ((1, 4),)),
    }


def layer_norm(values, gain):
    mean = lax.optimization_barrier(jnp.mean(values, axis=-1, keepdims=True))
    centered = values - mean
    var = lax.optimization_barrier(jnp.mean(centered * centered, axis=-1, keepdims=True))
    return centered * lax.rsqrt(var + 1e-05) * gain

def patch_block(x, ln1_gain, w_qkv, w_out, ln2_gain, w_fc1, w_fc2):
    head_dim = C // HEADS
    normed = layer_norm(x.astype(jnp.float32), ln1_gain).astype(jnp.bfloat16)
    qkv = jnp.einsum('rc,tcd->trd', normed.astype(jnp.float32), w_qkv.astype(jnp.float32)).astype(jnp.bfloat16)
    query = qkv[0].reshape(PATCH, HEADS, head_dim).astype(jnp.float32)
    keys = qkv[1].reshape(PATCH, HEADS, head_dim).astype(jnp.float32)
    values = qkv[2].reshape(PATCH, HEADS, head_dim).astype(jnp.float32)
    scores = jnp.einsum('qhd,khd->hqk', query, keys) / jnp.sqrt(jnp.float32(head_dim))
    probs = jax.nn.softmax(scores, axis=-1).astype(jnp.bfloat16)
    attn = jnp.einsum('hqk,khd->qhd', probs.astype(jnp.float32), values).astype(jnp.bfloat16).reshape(PATCH, C)
    mid = (x.astype(jnp.float32) + jnp.dot(attn, w_out, preferred_element_type=jnp.float32)).astype(jnp.bfloat16)
    normed2 = layer_norm(mid.astype(jnp.float32), ln2_gain).astype(jnp.bfloat16)
    act = jax.nn.gelu(jnp.dot(normed2, w_fc1, preferred_element_type=jnp.float32), approximate=False).astype(jnp.bfloat16)
    return (mid.astype(jnp.float32) + jnp.dot(act, w_fc2, preferred_element_type=jnp.float32)).astype(jnp.bfloat16)

def reference(feats, dest_pos, cell_id, ln1_gain, w_qkv, w_out, ln2_gain, w_fc1, w_fc2, w_pool):
    ordered = jnp.zeros_like(feats).at[dest_pos].set(feats)
    patches = ordered.reshape(NPTS // PATCH, PATCH, C)
    block_out = lax.map(lambda x: patch_block(x, ln1_gain, w_qkv, w_out, ln2_gain, w_fc1, w_fc2), patches).reshape(NPTS, C)
    lin = jnp.dot(block_out, w_pool, preferred_element_type=jnp.float32)
    sums = jax.ops.segment_sum(lin, cell_id, NCELL)
    counts = jax.ops.segment_sum(jnp.ones((NPTS,), jnp.float32), cell_id, NCELL)
    pooled = jax.nn.gelu(sums / counts[:, None], approximate=False).astype(jnp.bfloat16)
    return (block_out, pooled)
```

```python
import jax
import jax.numpy as jnp
from jax import lax
from jax.experimental import pallas as pl
from jax.experimental.pallas import tpu as pltpu
from jax.sharding import PartitionSpec as P

F32 = jnp.float32
BF16 = jnp.bfloat16

N_PTS = 128
N_CHAN = 4
ROWS = 1024
C = 512
LANES = 128
HEADS_HERE = 8
HEAD_DIM = 16
QUARTER = ROWS // N_CHAN
CELLS = ROWS // 8
CAP = 192
BLOCK = CAP + 16
KINDS = 8
SLOTS = KINDS * CAP
HALF = 256
WROWS = 768
MESSAGE = QUARTER + 3 * CELLS
VMEM_LIMIT = 48 * 1024 * 1024


def chip_up(i):
    return (i + 2 if (i >> 1) % 2 == 0 else i - 2) % N_PTS


def chip_down(i):
    return (i - 2 if (i >> 1) % 2 == 0 else i + 2) % N_PTS


def core_swap(i):
    return i ^ 1


def next_pair(i):
    return (i - 1 if i % 2 == 0 else i + 1) % N_PTS


def far_pair(i):
    return (i - 3 if i % 2 == 0 else i + 3) % N_PTS


def across(i):
    return (i + N_PTS // 2) % N_PTS


def exchange(x, partner):
    return lax.ppermute(x, "pts", [(i, partner(i)) for i in range(N_PTS)])


def offsets_of(me):
    core = lax.rem(me, 2)
    chip = lax.rem(me // 2, 2)
    up = 2 - 4 * chip
    swap = 1 - 2 * core
    return [0 * me, up, up + swap, -up, swap - up, swap, 6 * core - 3, 0 * me + 64]


def matmul(a, b):
    return jnp.dot(a, b, preferred_element_type=F32)


def matmul_nt(a, b):
    return lax.dot_general(a, b, (((1,), (1,)), ((), ())), preferred_element_type=F32)


def matmul_tn(a, b):
    return lax.dot_general(a, b, (((0,), (0,)), ((), ())), preferred_element_type=F32)


def one_hot(row, height):
    index = lax.broadcasted_iota(jnp.int32, (height, row.shape[1]), 0)
    return jnp.where(index == row, 1.0, 0.0).astype(BF16)


def gelu(x):
    return 0.5 * x * (1.0 + lax.erf(x * 0.7071067811865476))


def normed_chunks(chunks, gains):
    total = chunks[0]
    for x in chunks[1:]:
        total = total + x
    mean = jnp.sum(total, axis=-1, keepdims=True) * (1.0 / C)
    centered = [x - mean for x in chunks]
    square = centered[0] * centered[0]
    for x in centered[1:]:
        square = square + x * x
    var = jnp.sum(square, axis=-1, keepdims=True) * (1.0 / C)
    scale = lax.rsqrt(var + 1e-05)
    return [(x * scale * g).astype(BF16) for x, g in zip(centered, gains)]


def pack_kernel(
    feats_ref, dest_ref, cell_ref, w_out_ref, w_fc1_ref, w_fc2_ref, w_pool_ref,
    own_ref, up_ref, down_ref, swap_ref, far_ref, across_ref, weights_ref,
):
    me = lax.axis_index("pts")
    core = lax.rem(me, 2)

    for side in range(2):

        @pl.when(core == side)
        def _():
            cols = slice(side * HALF, (side + 1) * HALF)
            weights_ref[0:256, 0:256] = w_fc1_ref[0:256, cols]
            weights_ref[0:256, 256:512] = w_fc1_ref[256:512, cols]
            weights_ref[256:512, :] = w_fc2_ref[cols, :]

    weights_ref[512:640, :] = w_out_ref[...]
    for r in range(4):
        weights_ref[640:768, r * 128 : (r + 1) * 128] = w_pool_ref[r * 128 : (r + 1) * 128, :]

    offsets = offsets_of(me)
    dest = dest_ref[...]
    away = ((dest >> 10) - me) & (N_PTS - 1)
    local = dest & (ROWS - 1)
    kind = jnp.zeros_like(dest)
    for m in range(1, KINDS):
        kind = jnp.where(away == (offsets[m] & (N_PTS - 1)), m, kind)

    kinds = one_hot(kind, 16)
    before = lax.broadcasted_iota(jnp.int32, (ROWS, ROWS), 0)
    after = lax.broadcasted_iota(jnp.int32, (ROWS, ROWS), 1)
    earlier = jnp.where(before < after, 1.0, 0.0).astype(BF16)
    ranks = matmul(kinds, earlier) * kinds.astype(F32)
    rank = jnp.sum(ranks, axis=0, keepdims=True).astype(jnp.int32)
    slot = jnp.where(rank < 128, kind * 128 + rank, 1024 - 128 + kind * 64 + rank)

    chosen = one_hot(slot, SLOTS)
    packed = matmul(chosen, feats_ref[...]).astype(BF16)
    line = lax.broadcasted_iota(jnp.int32, (16, ROWS), 0)
    digits = jnp.where(line == 0, (local >> 5) + 1, jnp.where(line == 1, local & 31, 0))
    places = matmul_nt(digits.astype(F32).astype(BF16), chosen)

    relative = cell_ref[...] - (me - 1) * CELLS
    counts = matmul_nt(jnp.full((16, ROWS), 1.0, BF16), one_hot(relative, 3 * CELLS))
    counts = counts[0:1, :].astype(jnp.int32)

    small = lax.broadcasted_iota(jnp.int32, (16, 128), 0)
    lane = lax.broadcasted_iota(jnp.int32, (1, 128), 1)
    homes = [
        (own_ref, 0), (up_ref, 0), (up_ref, BLOCK), (down_ref, 0),
        (down_ref, BLOCK), (swap_ref, 0), (far_ref, 0), (across_ref, 0),
    ]
    for m, (ref, base) in enumerate(homes):
        ref[base : base + 128, :] = packed[m * 128 : (m + 1) * 128, :]
        ref[base + 128 : base + CAP, :] = packed[1024 + m * 64 : 1024 + (m + 1) * 64, :]
        first = places[0:2, m * 128 : (m + 1) * 128]
        mine = (lane >= 64) if m % 2 else (lane < 64)
        tile = 1024 + (m // 2) * 128
        second = jnp.where(mine, places[0:2, tile : tile + 128], 0.0)
        if m == 0:
            count = counts[:, CELLS : 2 * CELLS]
        else:
            ahead = (offsets[m] == 1).astype(jnp.int32)
            behind = (offsets[m] == -1).astype(jnp.int32)
            count = counts[:, 2 * CELLS :] * ahead + counts[:, :CELLS] * behind
        rows = [
            first[0:1], first[1:2], second[0:1], second[1:2],
            (count >> 5).astype(F32), (count & 31).astype(F32),
        ]
        notes = jnp.zeros((16, 128), F32)
        for r, value in enumerate(rows):
            notes = jnp.where(small == r, value, notes)
        ref[base + CAP : base + BLOCK, :] = notes.astype(BF16)


def unpack_kernel(own_ref, up_ref, down_ref, far_ref, across_ref, swap_ref, out_ref, count_ref, held):
    homes = [
        (own_ref, 0), (up_ref, 0), (swap_ref, BLOCK), (down_ref, 0),
        (swap_ref, 2 * BLOCK), (swap_ref, 0), (far_ref, 0), (across_ref, 0),
    ]
    firsts, seconds = [], []
    count = jnp.zeros((1, 128), F32)
    for m, (ref, base) in enumerate(homes):
        held[m * 128 : (m + 1) * 128, :] = ref[base : base + 128, :]
        held[1024 + m * 64 : 1024 + (m + 1) * 64, :] = ref[base + 128 : base + CAP, :]
        notes = ref[base + CAP : base + BLOCK, :].astype(F32)
        firsts.append(notes[0:1] * 32.0 + notes[1:2] - 32.0)
        seconds.append(notes[2:3] * 32.0 + notes[3:4])
        count = count + notes[4:5] * 32.0 + notes[5:6]
    pairs = [seconds[m] + seconds[m + 1] - 32.0 for m in range(0, KINDS, 2)]
    places = jnp.concatenate(firsts + pairs, axis=1).astype(jnp.int32)
    ordered = matmul(one_hot(places, ROWS), held[...]).astype(BF16)
    for c in range(N_CHAN):
        out_ref[c * ROWS : (c + 1) * ROWS, :] = ordered
    count_ref[...] = jnp.broadcast_to(count, (128, 128)).T


def attention_kernel(x_ref, gain_ref, w_ref, out_ref, normed, q_ref, k_ref, v_ref):
    gains = [gain_ref[:, c * 128 : (c + 1) * 128] for c in range(4)]
    for r in range(4):
        rows = slice(r * 256, (r + 1) * 256)
        chunks = [x_ref[c * ROWS + r * 256 : c * ROWS + (r + 1) * 256, :].astype(F32) for c in range(4)]
        for c, part in enumerate(normed_chunks(chunks, gains)):
            normed[rows, c * 128 : (c + 1) * 128] = part
    everything = normed[...]
    q_ref[...] = (matmul(everything, w_ref[0]).astype(BF16).astype(F32) * 0.25).astype(BF16)
    k_ref[...] = matmul(everything, w_ref[1]).astype(BF16)
    v_ref[...] = matmul(everything, w_ref[2]).T.astype(BF16)
    head_of = lax.broadcasted_iota(jnp.int32, (256, LANES), 1) // HEAD_DIM

    def head(h, carry):
        values = v_ref[pl.ds(pl.multiple_of(h * HEAD_DIM, HEAD_DIM), HEAD_DIM), :]
        for part in range(4):
            query = q_ref[part * 256 : (part + 1) * 256, :].astype(F32)
            query = jnp.where(head_of == h, query, 0.0).astype(BF16)
            scores = matmul_nt(k_ref[...], query)
            top = jnp.max(scores, axis=0, keepdims=True)
            grown = jnp.exp(scores - top)
            share = 1.0 / jnp.sum(grown, axis=0, keepdims=True)
            probs = (grown * share).astype(BF16)
            result = matmul(values, probs).astype(BF16)
            start = pl.multiple_of(part * 128 + h * HEAD_DIM, HEAD_DIM)
            out_ref[pl.ds(start, HEAD_DIM), :] = result
        return carry

    lax.fori_loop(0, HEADS_HERE, head, 0)


def mlp_kernel(
    attn_ref, x_ref, gain_ref, cell_ref, mine_ref, other_ref, out_ref,
    x_rows, w_out, w_fc1, w_fc2, w_pool, sems,
):
    chan = lax.axis_index("chan")
    me = lax.axis_index("pts")
    row = pl.multiple_of(chan * QUARTER, QUARTER)
    copies = []

    def start(group, src, dst):
        copy = pltpu.make_async_copy(src, dst, sems.at[len(copies)])
        copy.start()
        copies.append(copy)
        group.append(copy)

    def wait(group):
        for copy in group:
            copy.wait()

    early, late, stages = [], [], []
    for c in range(4):
        start(early, x_ref.at[pl.ds(c * ROWS + row, QUARTER), :], x_rows.at[:, c * 128 : (c + 1) * 128])
        start(early, mine_ref.at[c * WROWS + 512 : c * WROWS + 640, :], w_out.at[c * 128 : (c + 1) * 128, :])
    for s, ref in enumerate((mine_ref, other_ref)):
        for c in range(4):
            stage = []
            k = s * 4 + c
            base = c * WROWS
            start(stage, ref.at[base : base + 256, 0:256], w_fc1.at[k, 0:256, :])
            start(stage, ref.at[base : base + 256, 256:512], w_fc1.at[k, 256:512, :])
            start(stage, ref.at[base + 256 : base + 512, :], w_fc2.at[k])
            stages.append(stage)
    for c in range(4):
        for r in range(4):
            src = mine_ref.at[c * WROWS + 640 : c * WROWS + 768, r * 128 : (r + 1) * 128]
            start(late, src, w_pool.at[r * 128 : (r + 1) * 128, c * 128 : (c + 1) * 128])

    wait(early)
    mid = (x_rows[...].astype(F32) + matmul_tn(attn_ref[...], w_out[...])).astype(BF16)
    mid = mid.astype(F32)
    normed = normed_chunks([mid], [gain_ref[...]])[0]
    total = mid
    for k, stage in enumerate(stages):
        wait(stage)
        act = gelu(matmul(normed, w_fc1[k])).astype(BF16)
        term = matmul(act, w_fc2[k])
        summed = term if k == 0 else summed + term
    block = (total + summed).astype(BF16)
    wait(late)
    lin = matmul(block, w_pool[...])
    high = lin.astype(BF16)
    low = (lin - high.astype(F32)).astype(BF16)
    member = one_hot(cell_ref[pl.ds(chan, 1), :] - (me - 1) * CELLS, 3 * CELLS)
    sums = (matmul(member, high) + matmul(member, low)).astype(BF16)
    for c in range(4):
        cols = slice(c * 128, (c + 1) * 128)
        out_ref[c * MESSAGE : c * MESSAGE + QUARTER, :] = block[:, cols]
        out_ref[c * MESSAGE + QUARTER : (c + 1) * MESSAGE, :] = sums[:, cols]


def gather_kernel(got_ref, block_ref, own_ref, swap_ref, next_ref):
    core = lax.rem(lax.axis_index("pts"), 2)
    sums = jnp.zeros((3 * CELLS, LANES), F32)
    for c in range(4):
        block_ref[c * QUARTER : (c + 1) * QUARTER, :] = got_ref[c * MESSAGE : c * MESSAGE + QUARTER, :]
        sums = sums + got_ref[c * MESSAGE + QUARTER : (c + 1) * MESSAGE, :].astype(F32)
    own_ref[...] = sums[CELLS : 2 * CELLS]
    before = sums[:CELLS].astype(BF16)
    after = sums[2 * CELLS :].astype(BF16)

    @pl.when(core == 0)
    def _():
        swap_ref[...] = after
        next_ref[...] = before

    @pl.when(core == 1)
    def _():
        swap_ref[...] = before
        next_ref[...] = after


def pool_kernel(own_ref, swap_ref, next_ref, count_ref, out_ref):
    total = own_ref[...] + swap_ref[...].astype(F32) + next_ref[...].astype(F32)
    out_ref[...] = gelu(total / count_ref[...]).astype(BF16)


def call(kernel, outs, args, scratch=(), anywhere=(), flops=0, bytes_accessed=0):
    vmem = pl.BlockSpec(memory_space=pltpu.VMEM)
    return pl.pallas_call(
        kernel,
        out_shape=[jax.ShapeDtypeStruct(shape, dtype) for shape, dtype in outs],
        in_specs=[pl.BlockSpec(memory_space=pl.ANY) if i in anywhere else vmem for i in range(len(args))],
        out_specs=[vmem] * len(outs),
        scratch_shapes=list(scratch),
        compiler_params=pltpu.CompilerParams(vmem_limit_bytes=VMEM_LIMIT),
    )(*args)


def body(feats, dest_pos, cell_id, ln1_gain, w_qkv, w_out, ln2_gain, w_fc1, w_fc2, w_pool):
    def block(count=1):
        return ((count * BLOCK, LANES), BF16)

    own, up, down, swap, far, over, weights = call(
        pack_kernel,
        [block(), block(2), block(2), block(), block(), block(), ((WROWS, C), BF16)],
        (feats, dest_pos.reshape(1, ROWS), cell_id.reshape(1, ROWS), w_out, w_fc1, w_fc2, w_pool),
    )
    gathered = lax.all_gather(weights, "chan", axis=0, tiled=True)
    up = exchange(up, chip_up)
    down = exchange(down, chip_down)
    far = exchange(far, far_pair)
    over = exchange(over, across)
    swap = exchange(jnp.concatenate([swap, up[BLOCK:], down[BLOCK:]], axis=0), core_swap)
    ordered, count = call(
        unpack_kernel,
        [((N_CHAN * ROWS, LANES), BF16), ((128, 128), F32)],
        (own, up, down, far, over, swap),
        scratch=[pltpu.VMEM((SLOTS, LANES), BF16)],
    )
    full = lax.all_to_all(ordered, "chan", split_axis=0, concat_axis=0, tiled=True)
    (attn,) = call(
        attention_kernel,
        [((N_CHAN * LANES, QUARTER), BF16)],
        (full, ln1_gain.reshape(1, C), w_qkv),
        scratch=[
            pltpu.VMEM((ROWS, C), BF16),
            pltpu.VMEM((ROWS, LANES), BF16),
            pltpu.VMEM((ROWS, LANES), BF16),
            pltpu.VMEM((LANES, ROWS), BF16),
        ],
    )
    attn, gathered = lax.optimization_barrier((attn, gathered))
    others = exchange(gathered, core_swap)
    attn = lax.all_to_all(attn, "chan", split_axis=0, concat_axis=0, tiled=True)
    (message,) = call(
        mlp_kernel,
        [((N_CHAN * MESSAGE, LANES), BF16)],
        (attn, full, ln2_gain.reshape(1, C), cell_id.reshape(N_CHAN, QUARTER), gathered, others),
        anywhere=(1, 4, 5),
        scratch=[
            pltpu.VMEM((QUARTER, C), BF16),
            pltpu.VMEM((C, C), BF16),
            pltpu.VMEM((8, C, HALF), BF16),
            pltpu.VMEM((8, HALF, C), BF16),
            pltpu.VMEM((C, C), BF16),
            pltpu.SemaphoreType.DMA((48,)),
        ],
    )
    got = lax.all_to_all(message, "chan", split_axis=0, concat_axis=0, tiled=True)
    cell_sum = ((CELLS, LANES), BF16)
    block_out, mine, for_swap, for_next = call(
        gather_kernel,
        [((ROWS, LANES), BF16), ((CELLS, LANES), F32), cell_sum, cell_sum],
        (got,),
    )
    from_swap = exchange(for_swap, core_swap)
    from_next = exchange(for_next, next_pair)
    (pooled,) = call(pool_kernel, [cell_sum], (mine, from_swap, from_next, count))
    return (block_out, pooled)


def solution(mesh):
    return jax.shard_map(
        body,
        mesh=mesh,
        in_specs=(
            P("pts", "chan"),
            P("pts"),
            P("pts"),
            P(),
            P(None, None, "chan"),
            P("chan", None),
            P(),
            P(None, "chan"),
            P("chan", None),
            P(None, "chan"),
        ),
        out_specs=(P("pts", "chan"), P("pts", "chan")),
        check_vma=False,
    )
```

```python
import jax
import jax.numpy as jnp
from jax import lax
from jax.experimental import pallas as pl
from jax.experimental.pallas import tpu as pltpu
from jax.sharding import PartitionSpec as P

F32 = jnp.float32
BF16 = jnp.bfloat16

N_PTS = 128
N_CHAN = 4
ROWS = 1024
C = 512
LANES = 128
HEADS_HERE = 8
HEAD_DIM = 16
QUARTER = ROWS // N_CHAN
CELLS = ROWS // 8
CAP = 192
BLOCK = CAP + 16
KINDS = 8
SLOTS = KINDS * CAP
HALF = 256
STEP = 512
FC1, FC2, POOL, WROWS = 256, 1280, 2304, 2560
MESSAGE = QUARTER + 3 * CELLS
VMEM_LIMIT = 48 * 1024 * 1024
MOST_VMEM = 61 * 1024 * 1024 + 512 * 1024
ALL_VMEM = 63 * 1024 * 1024 + 512 * 1024


def chip_up(i):
    return (i + 2 if (i >> 1) % 2 == 0 else i - 2) % N_PTS


def chip_down(i):
    return (i - 2 if (i >> 1) % 2 == 0 else i + 2) % N_PTS


def core_swap(i):
    return i ^ 1


def next_pair(i):
    return (i - 1 if i % 2 == 0 else i + 1) % N_PTS


def far_pair(i):
    return (i - 3 if i % 2 == 0 else i + 3) % N_PTS


def across(i):
    return (i + N_PTS // 2) % N_PTS


def exchange(x, partner):
    return lax.ppermute(x, "pts", [(i, partner(i)) for i in range(N_PTS)])


def offsets_of(me):
    core = lax.rem(me, 2)
    chip = lax.rem(me // 2, 2)
    up = 2 - 4 * chip
    swap = 1 - 2 * core
    return [0 * me, up, up + swap, -up, swap - up, swap, 6 * core - 3, 0 * me + 64]


def matmul(a, b):
    return jnp.dot(a, b, preferred_element_type=F32)


def matmul_nt(a, b):
    return lax.dot_general(a, b, (((1,), (1,)), ((), ())), preferred_element_type=F32)


def matmul_tn(a, b):
    return lax.dot_general(a, b, (((0,), (0,)), ((), ())), preferred_element_type=F32)


def one_hot(row, height):
    index = lax.broadcasted_iota(jnp.int32, (height, row.shape[1]), 0)
    return jnp.where(index == row, 1.0, 0.0).astype(BF16)


def gelu(x):
    return 0.5 * x * (1.0 + lax.erf(x * 0.7071067811865476))


def normed_chunks(chunks, gains):
    total = chunks[0]
    for x in chunks[1:]:
        total = total + x
    mean = jnp.sum(total, axis=-1, keepdims=True) * (1.0 / C)
    centered = [x - mean for x in chunks]
    square = centered[0] * centered[0]
    for x in centered[1:]:
        square = square + x * x
    var = jnp.sum(square, axis=-1, keepdims=True) * (1.0 / C)
    scale = lax.rsqrt(var + 1e-05)
    return [(x * scale * g).astype(BF16) for x, g in zip(centered, gains)]


def copier(sems):
    copies = []

    def start(src, dst):
        copy = pltpu.make_async_copy(src, dst, sems.at[len(copies)])
        copy.start()
        copies.append(copy)
        return copy

    return start


def wait(copies):
    for copy in copies:
        copy.wait()


def digits_of(dest):
    local = dest & (ROWS - 1)
    line = lax.broadcasted_iota(jnp.int32, (16, ROWS), 0)
    digits = jnp.where(line == 0, (local >> 5) + 1, jnp.where(line == 1, local & 31, 0))
    return digits.astype(F32).astype(BF16)


def cell_counts(cell, me):
    relative = cell - (me - 1) * CELLS
    counts = matmul_nt(jnp.full((16, ROWS), 1.0, BF16), one_hot(relative, 3 * CELLS))
    return counts[0:1, :].astype(jnp.int32)


def write_blocks(slot, dest, feats, blocks, counts):
    small = lax.broadcasted_iota(jnp.int32, (16, 128), 0)
    lane = lax.broadcasted_iota(jnp.int32, (1, 128), 1)
    chosen = one_hot(slot, SLOTS)
    packed = matmul(chosen, feats).astype(BF16)
    places = matmul_nt(digits_of(dest), chosen)
    for m, (ref, base, offset) in enumerate(blocks):
        ref[base : base + 128, :] = packed[m * 128 : (m + 1) * 128, :]
        ref[base + 128 : base + CAP, :] = packed[1024 + m * 64 : 1024 + (m + 1) * 64, :]
        first = places[0:2, m * 128 : (m + 1) * 128]
        mine = (lane >= 64) if m % 2 else (lane < 64)
        tile = 1024 + (m // 2) * 128
        second = jnp.where(mine, places[0:2, tile : tile + 128], 0.0)
        count = jnp.zeros((1, CELLS), jnp.int32)
        for away in (-1, 0, 1):
            near = jnp.where(offset == away, 1, 0)
            count = count + counts[:, (away + 1) * CELLS : (away + 2) * CELLS] * near
        rows = [
            first[0:1], first[1:2], second[0:1], second[1:2],
            (count >> 5).astype(F32), (count & 31).astype(F32),
        ]
        notes = jnp.zeros((16, 128), F32)
        for r, value in enumerate(rows):
            notes = jnp.where(small == r, value, notes)
        ref[base + CAP : base + BLOCK, :] = notes.astype(BF16)


def pack_kernel(
    feats_ref, dest_ref, cell_ref, w_out_ref, w_fc1_ref, w_fc2_ref, w_pool_ref,
    own_ref, up_ref, down_ref, swap_ref, far_ref, across_ref, weights_ref,
    feats_here, dest_here, cell_here, sems,
):
    me = lax.axis_index("pts")
    core = lax.rem(me, 2)
    start = copier(sems)
    dest_copy = start(dest_ref, dest_here)
    cell_copy = start(cell_ref, cell_here)
    feats_copy = start(feats_ref, feats_here)

    half = pl.multiple_of(core * HALF, HALF)
    quarter = pl.multiple_of(core * 64, 64)
    weight_copies = []
    for r in range(2):
        src = w_fc1_ref.at[:, pl.ds(pl.multiple_of(half + r * 128, 128), 128)]
        weight_copies.append(start(src, weights_ref.at[FC1 + r * C : FC1 + (r + 1) * C, :]))
    for r in range(4):
        cols = slice(r * 128, (r + 1) * 128)
        dst = weights_ref.at[FC2 + r * HALF : FC2 + (r + 1) * HALF, :]
        weight_copies.append(start(w_fc2_ref.at[pl.ds(half, HALF), cols], dst))
        dst = weights_ref.at[r * 64 : (r + 1) * 64, :]
        weight_copies.append(start(w_out_ref.at[pl.ds(quarter, 64), cols], dst))
    weight_copies.append(start(w_pool_ref.at[pl.ds(half, HALF), :], weights_ref.at[POOL:WROWS, :]))

    before = lax.broadcasted_iota(jnp.int32, (ROWS, ROWS), 0)
    after = lax.broadcasted_iota(jnp.int32, (ROWS, ROWS), 1)
    earlier = jnp.where(before < after, 1.0, 0.0).astype(BF16)
    wait([dest_copy])
    offsets = offsets_of(me)
    dest = dest_here[...]
    away = ((dest >> 10) - me) & (N_PTS - 1)
    kind = jnp.zeros_like(dest)
    for m in range(1, KINDS):
        kind = jnp.where(away == (offsets[m] & (N_PTS - 1)), m, kind)

    kinds = one_hot(kind, 16)
    ranks = matmul(kinds, earlier) * kinds.astype(F32)
    rank = jnp.sum(ranks, axis=0, keepdims=True).astype(jnp.int32)
    slot = jnp.where(rank < 128, kind * 128 + rank, 1024 - 128 + kind * 64 + rank)
    homes = [
        (own_ref, 0), (up_ref, 0), (up_ref, BLOCK), (down_ref, 0),
        (down_ref, BLOCK), (swap_ref, 0), (far_ref, 0), (across_ref, 0),
    ]
    blocks = [home + (offset,) for home, offset in zip(homes, offsets)]
    wait([cell_copy])
    counts = cell_counts(cell_here[...], me)
    wait([feats_copy])
    write_blocks(slot, dest, feats_here[...], blocks, counts)
    wait(weight_copies)


def unpack_kernel(own_ref, up_ref, down_ref, far_ref, across_ref, swap_ref, out_ref, count_ref, held):
    homes = [
        (own_ref, 0), (up_ref, 0), (swap_ref, BLOCK), (down_ref, 0),
        (swap_ref, 2 * BLOCK), (swap_ref, 0), (far_ref, 0), (across_ref, 0),
    ]
    firsts, seconds = [], []
    count = jnp.zeros((1, 128), F32)
    for m, (ref, base) in enumerate(homes):
        held[m * 128 : (m + 1) * 128, :] = ref[base : base + 128, :]
        held[1024 + m * 64 : 1024 + (m + 1) * 64, :] = ref[base + 128 : base + CAP, :]
        notes = ref[base + CAP : base + BLOCK, :].astype(F32)
        firsts.append(notes[0:1] * 32.0 + notes[1:2] - 32.0)
        seconds.append(notes[2:3] * 32.0 + notes[3:4])
        count = count + notes[4:5] * 32.0 + notes[5:6]
    pairs = [seconds[m] + seconds[m + 1] - 32.0 for m in range(0, KINDS, 2)]
    places = jnp.concatenate(firsts + pairs, axis=1).astype(jnp.int32)
    ordered = matmul(one_hot(places, ROWS), held[...]).astype(BF16)
    for c in range(N_CHAN):
        out_ref[c * ROWS : (c + 1) * ROWS, :] = ordered
    count_ref[...] = jnp.broadcast_to(count, (128, 128)).T


def attention_kernel(x_ref, gain_ref, w_ref, out_ref, normed, q_ref, k_ref, v_ref):
    gains = [gain_ref[:, c * 128 : (c + 1) * 128] for c in range(4)]
    for r in range(4):
        rows = slice(r * 256, (r + 1) * 256)
        chunks = [x_ref[c * ROWS + r * 256 : c * ROWS + (r + 1) * 256, :].astype(F32) for c in range(4)]
        for c, part in enumerate(normed_chunks(chunks, gains)):
            normed[rows, c * 128 : (c + 1) * 128] = part
    everything = normed[...]
    q_ref[...] = (matmul(everything, w_ref[0]).astype(BF16).astype(F32) * 0.25).astype(BF16)
    k_ref[...] = matmul(everything, w_ref[1]).astype(BF16)
    v_ref[...] = matmul(everything, w_ref[2]).T.astype(BF16)
    head_of = lax.broadcasted_iota(jnp.int32, (STEP, LANES), 1) // HEAD_DIM
    work = [(h, part) for h in range(HEADS_HERE) for part in range(ROWS // STEP)]

    def scores_of(h, part):
        query = q_ref[part * STEP : (part + 1) * STEP, :].astype(F32)
        query = jnp.where(head_of == h, query, 0.0).astype(BF16)
        return matmul_nt(k_ref[...], query)

    scores = scores_of(*work[0])
    for n, (h, part) in enumerate(work):
        following = scores_of(*work[n + 1]) if n + 1 < len(work) else None
        top = jnp.max(scores, axis=0, keepdims=True)
        grown = jnp.exp(scores - top)
        share = 1.0 / jnp.sum(grown, axis=0, keepdims=True)
        probs = (grown * share).astype(BF16)
        result = matmul(v_ref[h * HEAD_DIM : (h + 1) * HEAD_DIM, :], probs).astype(BF16)
        for u in range(STEP // QUARTER):
            row = (part * (STEP // QUARTER) + u) * LANES + h * HEAD_DIM
            out_ref[row : row + HEAD_DIM, :] = result[:, u * QUARTER : (u + 1) * QUARTER]
        scores = following


def mlp_kernel(
    attn_ref, x_ref, gain_ref, cell_ref, mine_ref, other_ref, out_ref, x_rows, held, sems,
):
    chan = lax.axis_index("chan")
    me = lax.axis_index("pts")
    core = lax.rem(me, 2)
    row = pl.multiple_of(chan * QUARTER, QUARTER)
    start = copier(sems)
    sources = [(s, c) for s in range(2) for c in range(4)]
    refs = (mine_ref, other_ref)
    early, late = [], []
    for c in range(4):
        src = x_ref.at[pl.ds(c * ROWS + row, QUARTER), :]
        early.append(start(src, x_rows.at[:, c * 128 : (c + 1) * 128]))
    for s, c in sources:
        early.append(start(refs[s].at[c * WROWS : c * WROWS + FC1, :], held.at[s, c, 0:FC1, :]))
    for s, c in sources:
        src = refs[s].at[c * WROWS + FC1 : (c + 1) * WROWS, :]
        late.append(start(src, held.at[s, c, FC1:WROWS, :]))

    def part(s, c, row, height, count):
        pieces = [held[s, c, row + r * height : row + (r + 1) * height, :] for r in range(count)]
        return jnp.concatenate(pieces, axis=1)

    wait(early)
    halves = (core, 1 - core)
    attn = jnp.concatenate(
        [attn_ref[pl.ds(pl.multiple_of(c * 128 + halves[s] * 64, 64), 64), :] for s, c in sources], axis=0
    )
    w_out = jnp.concatenate([part(s, c, 0, 64, 4) for s, c in sources], axis=0)
    mid = (x_rows[...].astype(F32) + matmul_tn(attn, w_out)).astype(BF16).astype(F32)
    normed = normed_chunks([mid], [gain_ref[...]])[0]
    summed = None
    for k, (s, c) in enumerate(sources):
        wait([late[k]])
        act = gelu(matmul(normed, part(s, c, FC1, C, 2))).astype(BF16)
        term = matmul(act, part(s, c, FC2, HALF, 4))
        summed = term if summed is None else summed + term
    block = (mid + summed).astype(BF16)
    left, right = block[:, :HALF].astype(F32), block[:, HALF:].astype(F32)
    lin = None
    for s in range(2):
        mine = jnp.where(halves[s] == 0, left, right).astype(BF16)
        w_pool = jnp.concatenate([held[s, c, POOL:WROWS, :] for c in range(4)], axis=1)
        term = matmul(mine, w_pool)
        lin = term if lin is None else lin + term
    high = lin.astype(BF16)
    low = (lin - high.astype(F32)).astype(BF16)
    member = one_hot(cell_ref[pl.ds(chan, 1), :] - (me - 1) * CELLS, 3 * CELLS)
    sums = (matmul(member, high) + matmul(member, low)).astype(BF16)
    for c in range(4):
        cols = slice(c * 128, (c + 1) * 128)
        out_ref[c * MESSAGE : c * MESSAGE + QUARTER, :] = block[:, cols]
        out_ref[c * MESSAGE + QUARTER : (c + 1) * MESSAGE, :] = sums[:, cols]


def gather_kernel(got_ref, block_ref, own_ref, swap_ref, next_ref):
    core = lax.rem(lax.axis_index("pts"), 2)
    sums = jnp.zeros((3 * CELLS, LANES), F32)
    for c in range(4):
        block_ref[c * QUARTER : (c + 1) * QUARTER, :] = got_ref[c * MESSAGE : c * MESSAGE + QUARTER, :]
        sums = sums + got_ref[c * MESSAGE + QUARTER : (c + 1) * MESSAGE, :].astype(F32)
    own_ref[...] = sums[CELLS : 2 * CELLS]
    before = sums[:CELLS].astype(BF16)
    after = sums[2 * CELLS :].astype(BF16)

    @pl.when(core == 0)
    def _():
        swap_ref[...] = after
        next_ref[...] = before

    @pl.when(core == 1)
    def _():
        swap_ref[...] = before
        next_ref[...] = after


def pool_kernel(own_ref, swap_ref, next_ref, count_ref, out_ref):
    total = own_ref[...] + swap_ref[...].astype(F32) + next_ref[...].astype(F32)
    out_ref[...] = gelu(total / count_ref[...]).astype(BF16)


def call(kernel, outs, args, scratch=(), in_hbm=(), out_hbm=(), limit=VMEM_LIMIT):
    vmem = pl.BlockSpec(memory_space=pltpu.VMEM)
    hbm = pl.BlockSpec(memory_space=pltpu.HBM)
    return pl.pallas_call(
        kernel,
        out_shape=[jax.ShapeDtypeStruct(shape, dtype) for shape, dtype in outs],
        in_specs=[hbm if i in in_hbm else vmem for i in range(len(args))],
        out_specs=[hbm if i in out_hbm else vmem for i in range(len(outs))],
        scratch_shapes=list(scratch),
        compiler_params=pltpu.CompilerParams(vmem_limit_bytes=limit),
    )(*args)


def body(feats, dest_pos, cell_id, ln1_gain, w_qkv, w_out, ln2_gain, w_fc1, w_fc2, w_pool):
    def block(count=1):
        return ((count * BLOCK, LANES), BF16)

    own, up, down, swap, far, over, weights = call(
        pack_kernel,
        [block(), block(2), block(2), block(), block(), block(), ((WROWS, LANES), BF16)],
        (feats, dest_pos.reshape(1, ROWS), cell_id.reshape(1, ROWS), w_out, w_fc1, w_fc2, w_pool),
        scratch=[
            pltpu.VMEM((ROWS, LANES), BF16),
            pltpu.VMEM((1, ROWS), jnp.int32),
            pltpu.VMEM((1, ROWS), jnp.int32),
            pltpu.SemaphoreType.DMA((14,)),
        ],
        limit=ALL_VMEM,
        in_hbm=range(7),
        out_hbm=(6,),
    )
    gathered = lax.all_gather(weights, "chan", axis=0, tiled=True)
    far = exchange(far, far_pair)
    over = exchange(over, across)
    up = exchange(up, chip_up)
    down = exchange(down, chip_down)
    swap, far, over = lax.optimization_barrier((swap, far, over))
    swap = exchange(jnp.concatenate([swap, up[BLOCK:], down[BLOCK:]], axis=0), core_swap)
    ordered, count = call(
        unpack_kernel,
        [((N_CHAN * ROWS, LANES), BF16), ((128, 128), F32)],
        (own, up, down, far, over, swap),
        scratch=[pltpu.VMEM((SLOTS, LANES), BF16)],
    )
    full = lax.all_to_all(ordered, "chan", split_axis=0, concat_axis=0, tiled=True)
    (attn,) = call(
        attention_kernel,
        [((N_CHAN * LANES, QUARTER), BF16)],
        (full, ln1_gain.reshape(1, C), w_qkv),
        scratch=[
            pltpu.VMEM((ROWS, C), BF16),
            pltpu.VMEM((ROWS, LANES), BF16),
            pltpu.VMEM((ROWS, LANES), BF16),
            pltpu.VMEM((LANES, ROWS), BF16),
        ],
    )
    attn, gathered = lax.optimization_barrier((attn, gathered))
    others = exchange(gathered, core_swap)
    attn = lax.all_to_all(attn, "chan", split_axis=0, concat_axis=0, tiled=True)
    (message,) = call(
        mlp_kernel,
        [((N_CHAN * MESSAGE, LANES), BF16)],
        (attn, full, ln2_gain.reshape(1, C), cell_id.reshape(N_CHAN, QUARTER), gathered, others),
        limit=MOST_VMEM,
        in_hbm=(4, 5),
        scratch=[
            pltpu.VMEM((QUARTER, C), BF16),
            pltpu.VMEM((2, N_CHAN, WROWS, LANES), BF16),
            pltpu.SemaphoreType.DMA((20,)),
        ],
    )
    got = lax.all_to_all(message, "chan", split_axis=0, concat_axis=0, tiled=True)
    cell_sum = ((CELLS, LANES), BF16)
    block_out, mine, for_swap, for_next = call(
        gather_kernel,
        [((ROWS, LANES), BF16), ((CELLS, LANES), F32), cell_sum, cell_sum],
        (got,),
    )
    from_swap = exchange(for_swap, core_swap)
    from_next = exchange(for_next, next_pair)
    (pooled,) = call(pool_kernel, [cell_sum], (mine, from_swap, from_next, count))
    return (block_out, pooled)


def solution(mesh):
    return jax.shard_map(
        body,
        mesh=mesh,
        in_specs=(
            P("pts", "chan"),
            P("pts"),
            P("pts"),
            P(),
            P(None, None, "chan"),
            P("chan", None),
            P(),
            P(None, "chan"),
            P("chan", None),
            P(None, "chan"),
        ),
        out_specs=(P("pts", "chan"), P("pts", "chan")),
        check_vma=False,
    )
```

```python
import jax
import jax.numpy as jnp
from jax import lax
from jax.experimental import pallas as pl
from jax.experimental.pallas import tpu as pltpu
from jax.sharding import PartitionSpec as P

F32 = jnp.float32
BF16 = jnp.bfloat16

N_PTS = 128
N_CHAN = 4
ROWS = 1024
C = 512
LANES = 128
HEADS_HERE = 8
HEAD_DIM = 16
QUARTER = ROWS // N_CHAN
CELLS = ROWS // 8
CAP = 192
BLOCK = CAP + 16
KINDS = 8
SLOTS = KINDS * CAP
HALF = 256
STEP = 512
FC1, FC2, POOL, WROWS = 256, 1280, 2304, 2560
MESSAGE = QUARTER + CELLS
VMEM_LIMIT = 48 * 1024 * 1024
MOST_VMEM = 61 * 1024 * 1024 + 512 * 1024
ALL_VMEM = 63 * 1024 * 1024 + 512 * 1024


def chip_up(i):
    return (i + 2 if (i >> 1) % 2 == 0 else i - 2) % N_PTS


def chip_down(i):
    return (i - 2 if (i >> 1) % 2 == 0 else i + 2) % N_PTS


def core_swap(i):
    return i ^ 1


def next_pair(i):
    return (i - 1 if i % 2 == 0 else i + 1) % N_PTS


def far_pair(i):
    return (i - 3 if i % 2 == 0 else i + 3) % N_PTS


def across(i):
    return (i + N_PTS // 2) % N_PTS


def exchange(x, partner):
    return lax.ppermute(x, "pts", [(i, partner(i)) for i in range(N_PTS)])


def offsets_of(me):
    core = lax.rem(me, 2)
    chip = lax.rem(me // 2, 2)
    up = 2 - 4 * chip
    swap = 1 - 2 * core
    return [0 * me, up, up + swap, -up, swap - up, swap, 6 * core - 3, 0 * me + 64]


def matmul(a, b):
    return jnp.dot(a, b, preferred_element_type=F32)


def matmul_nt(a, b):
    return lax.dot_general(a, b, (((1,), (1,)), ((), ())), preferred_element_type=F32)


def matmul_tn(a, b):
    return lax.dot_general(a, b, (((0,), (0,)), ((), ())), preferred_element_type=F32)


def one_hot(row, height):
    index = lax.broadcasted_iota(jnp.int32, (height, row.shape[1]), 0)
    return jnp.where(index == row, 1.0, 0.0).astype(BF16)


def gelu(x):
    return 0.5 * x * (1.0 + lax.erf(x * 0.7071067811865476))


def normed_chunks(chunks, gains):
    total = chunks[0]
    for x in chunks[1:]:
        total = total + x
    mean = jnp.sum(total, axis=-1, keepdims=True) * (1.0 / C)
    centered = [x - mean for x in chunks]
    square = centered[0] * centered[0]
    for x in centered[1:]:
        square = square + x * x
    var = jnp.sum(square, axis=-1, keepdims=True) * (1.0 / C)
    scale = lax.rsqrt(var + 1e-05)
    return [(x * scale * g).astype(BF16) for x, g in zip(centered, gains)]


def copier(sems):
    copies = []

    def start(src, dst):
        copy = pltpu.make_async_copy(src, dst, sems.at[len(copies)])
        copy.start()
        copies.append(copy)
        return copy

    return start


def wait(copies):
    for copy in copies:
        copy.wait()


def digits_of(dest):
    local = dest & (ROWS - 1)
    line = lax.broadcasted_iota(jnp.int32, (16, ROWS), 0)
    digits = jnp.where(line == 0, (local >> 5) + 1, jnp.where(line == 1, local & 31, 0))
    return digits.astype(F32).astype(BF16)


def cell_counts(cell, me):
    relative = cell - (me - 1) * CELLS
    counts = matmul_nt(jnp.full((16, ROWS), 1.0, BF16), one_hot(relative, 3 * CELLS))
    return counts[0:1, :].astype(jnp.int32)


def write_blocks(slot, dest, feats, blocks, counts):
    small = lax.broadcasted_iota(jnp.int32, (16, 128), 0)
    lane = lax.broadcasted_iota(jnp.int32, (1, 128), 1)
    chosen = one_hot(slot, SLOTS)
    packed = matmul(chosen, feats).astype(BF16)
    places = matmul_nt(digits_of(dest), chosen)
    for m, (ref, base, offset) in enumerate(blocks):
        ref[base : base + 128, :] = packed[m * 128 : (m + 1) * 128, :]
        ref[base + 128 : base + CAP, :] = packed[1024 + m * 64 : 1024 + (m + 1) * 64, :]
        first = places[0:2, m * 128 : (m + 1) * 128]
        mine = (lane >= 64) if m % 2 else (lane < 64)
        tile = 1024 + (m // 2) * 128
        second = jnp.where(mine, places[0:2, tile : tile + 128], 0.0)
        count = jnp.zeros((1, CELLS), jnp.int32)
        for away in (-1, 0, 1):
            near = jnp.where(offset == away, 1, 0)
            count = count + counts[:, (away + 1) * CELLS : (away + 2) * CELLS] * near
        rows = [
            first[0:1], first[1:2], second[0:1], second[1:2],
            (count >> 5).astype(F32), (count & 31).astype(F32),
        ]
        notes = jnp.zeros((16, 128), F32)
        for r, value in enumerate(rows):
            notes = jnp.where(small == r, value, notes)
        ref[base + CAP : base + BLOCK, :] = notes.astype(BF16)


def pack_kernel(
    feats_ref, dest_ref, cell_ref, w_out_ref, w_fc1_ref, w_fc2_ref, w_pool_ref,
    up_ref, down_ref, swap_ref, far_ref, across_ref, weights_ref,
    feats_here, dest_here, cell_here, sems,
):
    me = lax.axis_index("pts")
    core = lax.rem(me, 2)
    start = copier(sems)
    dest_copy = start(dest_ref, dest_here)
    cell_copy = start(cell_ref, cell_here)
    feats_copy = start(feats_ref, feats_here)

    half = pl.multiple_of(core * HALF, HALF)
    quarter = pl.multiple_of(core * 64, 64)
    weight_copies = []
    for r in range(2):
        src = w_fc1_ref.at[:, pl.ds(pl.multiple_of(half + r * 128, 128), 128)]
        weight_copies.append(start(src, weights_ref.at[FC1 + r * C : FC1 + (r + 1) * C, :]))
    for r in range(4):
        cols = slice(r * 128, (r + 1) * 128)
        dst = weights_ref.at[FC2 + r * HALF : FC2 + (r + 1) * HALF, :]
        weight_copies.append(start(w_fc2_ref.at[pl.ds(half, HALF), cols], dst))
        dst = weights_ref.at[r * 64 : (r + 1) * 64, :]
        weight_copies.append(start(w_out_ref.at[pl.ds(quarter, 64), cols], dst))
    weight_copies.append(start(w_pool_ref.at[pl.ds(half, HALF), :], weights_ref.at[POOL:WROWS, :]))

    before = lax.broadcasted_iota(jnp.int32, (ROWS, ROWS), 0)
    after = lax.broadcasted_iota(jnp.int32, (ROWS, ROWS), 1)
    earlier = jnp.where(before < after, 1.0, 0.0).astype(BF16)
    wait([dest_copy])
    offsets = offsets_of(me)
    dest = dest_here[...]
    away = ((dest >> 10) - me) & (N_PTS - 1)
    kind = jnp.zeros_like(dest)
    for m in range(1, KINDS):
        kind = jnp.where(away == (offsets[m] & (N_PTS - 1)), m, kind)

    kinds = one_hot(kind, 16)
    ranks = matmul(kinds, earlier) * kinds.astype(F32)
    rank = jnp.sum(ranks, axis=0, keepdims=True).astype(jnp.int32)
    slot = jnp.where(rank < 128, kind * 128 + rank, 1024 - 128 + kind * 64 + rank)
    homes = [
        (swap_ref, BLOCK), (up_ref, 0), (up_ref, BLOCK), (down_ref, 0),
        (down_ref, BLOCK), (swap_ref, 0), (far_ref, 0), (across_ref, 0),
    ]
    blocks = [home + (offset,) for home, offset in zip(homes, offsets)]
    wait([cell_copy])
    counts = cell_counts(cell_here[...], me)
    wait([feats_copy])
    write_blocks(slot, dest, feats_here[...], blocks, counts)
    wait(weight_copies)


def unpack_kernel(sent_ref, up_ref, down_ref, far_ref, across_ref, swap_ref, out_ref, count_ref, held):
    homes = [
        (sent_ref, BLOCK), (up_ref, 0), (swap_ref, 2 * BLOCK), (down_ref, 0),
        (swap_ref, 3 * BLOCK), (swap_ref, 0), (far_ref, 0), (across_ref, 0),
    ]
    firsts, seconds = [], []
    count = jnp.zeros((1, 128), F32)
    for m, (ref, base) in enumerate(homes):
        held[m * 128 : (m + 1) * 128, :] = ref[base : base + 128, :]
        held[1024 + m * 64 : 1024 + (m + 1) * 64, :] = ref[base + 128 : base + CAP, :]
        notes = ref[base + CAP : base + BLOCK, :].astype(F32)
        firsts.append(notes[0:1] * 32.0 + notes[1:2] - 32.0)
        seconds.append(notes[2:3] * 32.0 + notes[3:4])
        count = count + notes[4:5] * 32.0 + notes[5:6]
    pairs = [seconds[m] + seconds[m + 1] - 32.0 for m in range(0, KINDS, 2)]
    places = jnp.concatenate(firsts + pairs, axis=1).astype(jnp.int32)
    ordered = matmul(one_hot(places, ROWS), held[...]).astype(BF16)
    for c in range(N_CHAN):
        out_ref[c * ROWS : (c + 1) * ROWS, :] = ordered
    count_ref[...] = jnp.broadcast_to(count, (128, 128)).T


def attention_kernel(x_ref, gain_ref, w_ref, out_ref, normed, q_ref, k_ref, v_ref):
    gains = [gain_ref[:, c * 128 : (c + 1) * 128] for c in range(4)]
    for r in range(4):
        rows = slice(r * 256, (r + 1) * 256)
        chunks = [x_ref[c * ROWS + r * 256 : c * ROWS + (r + 1) * 256, :].astype(F32) for c in range(4)]
        for c, part in enumerate(normed_chunks(chunks, gains)):
            normed[rows, c * 128 : (c + 1) * 128] = part
    everything = normed[...]
    q_ref[...] = (matmul(everything, w_ref[0]).astype(BF16).astype(F32) * 0.25).astype(BF16)
    k_ref[...] = matmul(everything, w_ref[1]).astype(BF16)
    v_ref[...] = matmul(everything, w_ref[2]).T.astype(BF16)
    head_of = lax.broadcasted_iota(jnp.int32, (STEP, LANES), 1) // HEAD_DIM
    work = [(h, part) for h in range(HEADS_HERE) for part in range(ROWS // STEP)]

    def scores_of(h, part):
        query = q_ref[part * STEP : (part + 1) * STEP, :].astype(F32)
        query = jnp.where(head_of == h, query, 0.0).astype(BF16)
        return matmul_nt(k_ref[...], query)

    scores = scores_of(*work[0])
    for n, (h, part) in enumerate(work):
        following = scores_of(*work[n + 1]) if n + 1 < len(work) else None
        top = jnp.max(scores, axis=0, keepdims=True)
        grown = jnp.exp(scores - top)
        share = 1.0 / jnp.sum(grown, axis=0, keepdims=True)
        probs = (grown * share).astype(BF16)
        result = matmul(v_ref[h * HEAD_DIM : (h + 1) * HEAD_DIM, :], probs).astype(BF16)
        for u in range(STEP // QUARTER):
            row = (part * (STEP // QUARTER) + u) * LANES + h * HEAD_DIM
            out_ref[row : row + HEAD_DIM, :] = result[:, u * QUARTER : (u + 1) * QUARTER]
        scores = following


def mlp_kernel(
    attn_ref, x_ref, gain_ref, cell_ref, mine_ref, other_ref,
    block_ref, own_ref, swap_ref, next_ref, x_rows, held, sems,
):
    chan = lax.axis_index("chan")
    me = lax.axis_index("pts")
    core = lax.rem(me, 2)
    row = pl.multiple_of(chan * QUARTER, QUARTER)
    start = copier(sems)
    sources = [(s, c) for s in range(2) for c in range(4)]
    refs = (mine_ref, other_ref)
    early, late = [], []
    for c in range(4):
        src = x_ref.at[pl.ds(c * ROWS + row, QUARTER), :]
        early.append(start(src, x_rows.at[:, c * 128 : (c + 1) * 128]))
    for s, c in sources:
        early.append(start(refs[s].at[c * WROWS : c * WROWS + FC1, :], held.at[s, c, 0:FC1, :]))
    for s, c in sources:
        src = refs[s].at[c * WROWS + FC1 : (c + 1) * WROWS, :]
        late.append(start(src, held.at[s, c, FC1:WROWS, :]))

    def part(s, c, row, height, count):
        pieces = [held[s, c, row + r * height : row + (r + 1) * height, :] for r in range(count)]
        return jnp.concatenate(pieces, axis=1)

    wait(early)
    halves = (core, 1 - core)
    attn = jnp.concatenate(
        [attn_ref[pl.ds(pl.multiple_of(c * 128 + halves[s] * 64, 64), 64), :] for s, c in sources], axis=0
    )
    w_out = jnp.concatenate([part(s, c, 0, 64, 4) for s, c in sources], axis=0)
    mid = (x_rows[...].astype(F32) + matmul_tn(attn, w_out)).astype(BF16).astype(F32)
    normed = normed_chunks([mid], [gain_ref[...]])[0]
    summed = None
    for k, (s, c) in enumerate(sources):
        wait([late[k]])
        act = gelu(matmul(normed, part(s, c, FC1, C, 2))).astype(BF16)
        term = matmul(act, part(s, c, FC2, HALF, 4))
        summed = term if summed is None else summed + term
    block = (mid + summed).astype(BF16)
    left, right = block[:, :HALF].astype(F32), block[:, HALF:].astype(F32)
    lin = None
    for s in range(2):
        mine = jnp.where(halves[s] == 0, left, right).astype(BF16)
        w_pool = jnp.concatenate([held[s, c, POOL:WROWS, :] for c in range(4)], axis=1)
        term = matmul(mine, w_pool)
        lin = term if lin is None else lin + term
    high = lin.astype(BF16)
    low = (lin - high.astype(F32)).astype(BF16)
    member = one_hot(cell_ref[:, pl.ds(row, QUARTER)] - (me - 1) * CELLS, 3 * CELLS)
    sums = matmul(member, high) + matmul(member, low)
    block_ref[...] = block
    own_ref[...] = sums[CELLS : 2 * CELLS]
    before = sums[:CELLS].astype(BF16)
    after = sums[2 * CELLS :].astype(BF16)

    @pl.when(core == 0)
    def _():
        swap_ref[...] = after
        next_ref[...] = before

    @pl.when(core == 1)
    def _():
        swap_ref[...] = before
        next_ref[...] = after


def message_kernel(block_ref, own_ref, swap_ref, next_ref, out_ref):
    sums = own_ref[...] + swap_ref[...].astype(F32) + next_ref[...].astype(F32)
    sums = sums.astype(BF16)
    for c in range(N_CHAN):
        cols = slice(c * 128, (c + 1) * 128)
        out_ref[c * MESSAGE : c * MESSAGE + QUARTER, :] = block_ref[:, cols]
        out_ref[c * MESSAGE + QUARTER : (c + 1) * MESSAGE, :] = sums[:, cols]


def pool_kernel(got_ref, count_ref, block_ref, out_ref):
    total = jnp.zeros((CELLS, LANES), F32)
    for c in range(N_CHAN):
        block_ref[c * QUARTER : (c + 1) * QUARTER, :] = got_ref[c * MESSAGE : c * MESSAGE + QUARTER, :]
        total = total + got_ref[c * MESSAGE + QUARTER : (c + 1) * MESSAGE, :].astype(F32)
    out_ref[...] = gelu(total / count_ref[...]).astype(BF16)


def call(kernel, outs, args, scratch=(), in_hbm=(), out_hbm=(), limit=VMEM_LIMIT):
    vmem = pl.BlockSpec(memory_space=pltpu.VMEM)
    hbm = pl.BlockSpec(memory_space=pltpu.HBM)
    return pl.pallas_call(
        kernel,
        out_shape=[jax.ShapeDtypeStruct(shape, dtype) for shape, dtype in outs],
        in_specs=[hbm if i in in_hbm else vmem for i in range(len(args))],
        out_specs=[hbm if i in out_hbm else vmem for i in range(len(outs))],
        scratch_shapes=list(scratch),
        compiler_params=pltpu.CompilerParams(vmem_limit_bytes=limit),
    )(*args)


def body(feats, dest_pos, cell_id, ln1_gain, w_qkv, w_out, ln2_gain, w_fc1, w_fc2, w_pool):
    def block(count=1):
        return ((count * BLOCK, LANES), BF16)

    up, down, swap, far, over, weights = call(
        pack_kernel,
        [block(2), block(2), block(2), block(), block(), ((WROWS, LANES), BF16)],
        (feats, dest_pos.reshape(1, ROWS), cell_id.reshape(1, ROWS), w_out, w_fc1, w_fc2, w_pool),
        scratch=[
            pltpu.VMEM((ROWS, LANES), BF16),
            pltpu.VMEM((1, ROWS), jnp.int32),
            pltpu.VMEM((1, ROWS), jnp.int32),
            pltpu.SemaphoreType.DMA((14,)),
        ],
        limit=ALL_VMEM,
        in_hbm=range(7),
    )
    gathered = lax.all_gather(weights, "chan", axis=0, tiled=True)
    far = exchange(far, far_pair)
    over = exchange(over, across)
    up = exchange(up, chip_up)
    down = exchange(down, chip_down)
    swap, far, over = lax.optimization_barrier((swap, far, over))
    sent = jnp.concatenate([swap, up[BLOCK:], down[BLOCK:]], axis=0)
    swap = exchange(sent, core_swap)
    ordered, count = call(
        unpack_kernel,
        [((N_CHAN * ROWS, LANES), BF16), ((128, 128), F32)],
        (sent, up, down, far, over, swap),
        scratch=[pltpu.VMEM((SLOTS, LANES), BF16)],
    )
    full = lax.all_to_all(ordered, "chan", split_axis=0, concat_axis=0, tiled=True)
    (attn,) = call(
        attention_kernel,
        [((N_CHAN * LANES, QUARTER), BF16)],
        (full, ln1_gain.reshape(1, C), w_qkv),
        scratch=[
            pltpu.VMEM((ROWS, C), BF16),
            pltpu.VMEM((ROWS, LANES), BF16),
            pltpu.VMEM((ROWS, LANES), BF16),
            pltpu.VMEM((LANES, ROWS), BF16),
        ],
    )
    attn, gathered = lax.optimization_barrier((attn, gathered))
    others = exchange(gathered, core_swap)
    attn = lax.all_to_all(attn, "chan", split_axis=0, concat_axis=0, tiled=True)
    cell_sum = ((CELLS, C), BF16)
    rows, mine, for_swap, for_next = call(
        mlp_kernel,
        [((QUARTER, C), BF16), ((CELLS, C), F32), cell_sum, cell_sum],
        (attn, full, ln2_gain.reshape(1, C), cell_id.reshape(1, ROWS), gathered, others),
        limit=MOST_VMEM,
        in_hbm=(4, 5),
        scratch=[
            pltpu.VMEM((QUARTER, C), BF16),
            pltpu.VMEM((2, N_CHAN, WROWS, LANES), BF16),
            pltpu.SemaphoreType.DMA((20,)),
        ],
    )
    from_swap = exchange(for_swap, core_swap)
    from_next = exchange(for_next, next_pair)
    (message,) = call(
        message_kernel,
        [((N_CHAN * MESSAGE, LANES), BF16)],
        (rows, mine, from_swap, from_next),
    )
    got = lax.all_to_all(message, "chan", split_axis=0, concat_axis=0, tiled=True)
    block_out, pooled = call(
        pool_kernel, [((ROWS, LANES), BF16), ((CELLS, LANES), BF16)], (got, count)
    )
    return (block_out, pooled)


def solution(mesh):
    return jax.shard_map(
        body,
        mesh=mesh,
        in_specs=(
            P("pts", "chan"),
            P("pts"),
            P("pts"),
            P(),
            P(None, None, "chan"),
            P("chan", None),
            P(),
            P(None, "chan"),
            P("chan", None),
            P(None, "chan"),
        ),
        out_specs=(P("pts", "chan"), P("pts", "chan")),
        check_vma=False,
    )
```

```python
import jax
import jax.numpy as jnp
from jax import lax
from jax.experimental import pallas as pl
from jax.experimental.pallas import tpu as pltpu
from jax.sharding import PartitionSpec as P

F32 = jnp.float32
BF16 = jnp.bfloat16

N_PTS = 128
N_CHAN = 4
ROWS = 1024
C = 512
LANES = 128
HEADS_HERE = 8
HEAD_DIM = 16
QUARTER = ROWS // N_CHAN
CELLS = ROWS // 8
CAP = 192
BLOCK = CAP + 16
KINDS = 8
SLOTS = KINDS * CAP
HALF = 256
STEP = 512
HALF_ROWS = 2048
SQUARE_ROWS = 1024
MESSAGE = QUARTER + CELLS
VMEM_LIMIT = 48 * 1024 * 1024
SOME_VMEM = 32 * 1024 * 1024
ALL_VMEM = 63 * 1024 * 1024 + 512 * 1024


def chip_up(i):
    return (i + 2 if (i >> 1) % 2 == 0 else i - 2) % N_PTS


def chip_down(i):
    return (i - 2 if (i >> 1) % 2 == 0 else i + 2) % N_PTS


def core_swap(i):
    return i ^ 1


def next_pair(i):
    return (i - 1 if i % 2 == 0 else i + 1) % N_PTS


def far_pair(i):
    return (i - 3 if i % 2 == 0 else i + 3) % N_PTS


def across(i):
    return (i + N_PTS // 2) % N_PTS


def exchange(x, partner):
    return lax.ppermute(x, "pts", [(i, partner(i)) for i in range(N_PTS)])


def offsets_of(me):
    core = lax.rem(me, 2)
    chip = lax.rem(me // 2, 2)
    up = 2 - 4 * chip
    swap = 1 - 2 * core
    return [0 * me, up, up + swap, -up, swap - up, swap, 6 * core - 3, 0 * me + 64]


def matmul(a, b):
    return jnp.dot(a, b, preferred_element_type=F32)


def matmul_nt(a, b):
    return lax.dot_general(a, b, (((1,), (1,)), ((), ())), preferred_element_type=F32)


def matmul_tn(a, b):
    return lax.dot_general(a, b, (((0,), (0,)), ((), ())), preferred_element_type=F32)


def one_hot(row, height):
    index = lax.broadcasted_iota(jnp.int32, (height, row.shape[1]), 0)
    return jnp.where(index == row, 1.0, 0.0).astype(BF16)


def gelu(x):
    return 0.5 * x * (1.0 + lax.erf(x * 0.7071067811865476))


def normed_chunks(chunks, gains):
    total = chunks[0]
    for x in chunks[1:]:
        total = total + x
    mean = jnp.sum(total, axis=-1, keepdims=True) * (1.0 / C)
    centered = [x - mean for x in chunks]
    square = centered[0] * centered[0]
    for x in centered[1:]:
        square = square + x * x
    var = jnp.sum(square, axis=-1, keepdims=True) * (1.0 / C)
    scale = lax.rsqrt(var + 1e-05)
    return [(x * scale * g).astype(BF16) for x, g in zip(centered, gains)]


def copier(sems):
    copies = []

    def start(src, dst):
        copy = pltpu.make_async_copy(src, dst, sems.at[len(copies)])
        copy.start()
        copies.append(copy)
        return copy

    return start


def wait(copies):
    for copy in copies:
        copy.wait()


def digits_of(dest):
    local = dest & (ROWS - 1)
    line = lax.broadcasted_iota(jnp.int32, (16, ROWS), 0)
    digits = jnp.where(line == 0, (local >> 5) + 1, jnp.where(line == 1, local & 31, 0))
    return digits.astype(F32).astype(BF16)


def cell_counts(cell, me):
    relative = cell - (me - 1) * CELLS
    counts = matmul_nt(jnp.full((16, ROWS), 1.0, BF16), one_hot(relative, 3 * CELLS))
    return counts[0:1, :].astype(jnp.int32)


def write_blocks(slot, dest, feats, blocks, counts):
    small = lax.broadcasted_iota(jnp.int32, (16, 128), 0)
    lane = lax.broadcasted_iota(jnp.int32, (1, 128), 1)
    chosen = one_hot(slot, SLOTS)
    packed = matmul(chosen, feats).astype(BF16)
    places = matmul_nt(digits_of(dest), chosen)
    for m, (ref, base, offset) in enumerate(blocks):
        ref[base : base + 128, :] = packed[m * 128 : (m + 1) * 128, :]
        ref[base + 128 : base + CAP, :] = packed[1024 + m * 64 : 1024 + (m + 1) * 64, :]
        first = places[0:2, m * 128 : (m + 1) * 128]
        mine = (lane >= 64) if m % 2 else (lane < 64)
        tile = 1024 + (m // 2) * 128
        second = jnp.where(mine, places[0:2, tile : tile + 128], 0.0)
        count = jnp.zeros((1, CELLS), jnp.int32)
        for away in (-1, 0, 1):
            near = jnp.where(offset == away, 1, 0)
            count = count + counts[:, (away + 1) * CELLS : (away + 2) * CELLS] * near
        rows = [
            first[0:1], first[1:2], second[0:1], second[1:2],
            (count >> 5).astype(F32), (count & 31).astype(F32),
        ]
        notes = jnp.zeros((16, 128), F32)
        for r, value in enumerate(rows):
            notes = jnp.where(small == r, value, notes)
        ref[base + CAP : base + BLOCK, :] = notes.astype(BF16)


def pack_kernel(
    feats_ref, dest_ref, cell_ref, w_out_ref, w_fc1_ref, w_fc2_ref, w_pool_ref,
    up_ref, down_ref, swap_ref, far_ref, across_ref, halves_ref, square_ref,
    feats_here, dest_here, cell_here, sems,
):
    me = lax.axis_index("pts")
    core = lax.rem(me, 2)
    start = copier(sems)
    dest_copy = start(dest_ref, dest_here)
    cell_copy = start(cell_ref, cell_here)
    feats_copy = start(feats_ref, feats_here)

    half = pl.multiple_of(core * HALF, HALF)
    weight_copies = []
    for r in range(2):
        src = w_fc1_ref.at[:, pl.ds(pl.multiple_of(half + r * 128, 128), 128)]
        weight_copies.append(start(src, halves_ref.at[r * C : (r + 1) * C, :]))
    for r in range(4):
        cols = slice(r * 128, (r + 1) * 128)
        dst = halves_ref.at[2 * C + r * HALF : 2 * C + (r + 1) * HALF, :]
        weight_copies.append(start(w_fc2_ref.at[pl.ds(half, HALF), cols], dst))
        weight_copies.append(start(w_out_ref.at[:, cols], square_ref.at[r * 128 : (r + 1) * 128, :]))
    weight_copies.append(start(w_pool_ref, square_ref.at[C:, :]))

    before = lax.broadcasted_iota(jnp.int32, (ROWS, ROWS), 0)
    after = lax.broadcasted_iota(jnp.int32, (ROWS, ROWS), 1)
    earlier = jnp.where(before < after, 1.0, 0.0).astype(BF16)
    wait([dest_copy])
    offsets = offsets_of(me)
    dest = dest_here[...]
    away = ((dest >> 10) - me) & (N_PTS - 1)
    kind = jnp.zeros_like(dest)
    for m in range(1, KINDS):
        kind = jnp.where(away == (offsets[m] & (N_PTS - 1)), m, kind)

    kinds = one_hot(kind, 16)
    ranks = matmul(kinds, earlier) * kinds.astype(F32)
    rank = jnp.sum(ranks, axis=0, keepdims=True).astype(jnp.int32)
    slot = jnp.where(rank < 128, kind * 128 + rank, 1024 - 128 + kind * 64 + rank)
    homes = [
        (swap_ref, BLOCK), (up_ref, 0), (up_ref, BLOCK), (down_ref, 0),
        (down_ref, BLOCK), (swap_ref, 0), (far_ref, 0), (across_ref, 0),
    ]
    blocks = [home + (offset,) for home, offset in zip(homes, offsets)]
    wait([cell_copy])
    counts = cell_counts(cell_here[...], me)
    wait([feats_copy])
    write_blocks(slot, dest, feats_here[...], blocks, counts)
    wait(weight_copies)


def unpack_kernel(sent_ref, up_ref, down_ref, far_ref, across_ref, swap_ref, out_ref, count_ref, held):
    homes = [
        (sent_ref, BLOCK), (up_ref, 0), (swap_ref, 2 * BLOCK), (down_ref, 0),
        (swap_ref, 3 * BLOCK), (swap_ref, 0), (far_ref, 0), (across_ref, 0),
    ]
    firsts, seconds = [], []
    count = jnp.zeros((1, 128), F32)
    for m, (ref, base) in enumerate(homes):
        held[m * 128 : (m + 1) * 128, :] = ref[base : base + 128, :]
        held[1024 + m * 64 : 1024 + (m + 1) * 64, :] = ref[base + 128 : base + CAP, :]
        notes = ref[base + CAP : base + BLOCK, :].astype(F32)
        firsts.append(notes[0:1] * 32.0 + notes[1:2] - 32.0)
        seconds.append(notes[2:3] * 32.0 + notes[3:4])
        count = count + notes[4:5] * 32.0 + notes[5:6]
    pairs = [seconds[m] + seconds[m + 1] - 32.0 for m in range(0, KINDS, 2)]
    places = jnp.concatenate(firsts + pairs, axis=1).astype(jnp.int32)
    ordered = matmul(one_hot(places, ROWS), held[...]).astype(BF16)
    for c in range(N_CHAN):
        out_ref[c * ROWS : (c + 1) * ROWS, :] = ordered
    count_ref[...] = jnp.broadcast_to(count, (128, 128)).T


def attention_kernel(x_ref, gain_ref, w_ref, out_ref, normed, q_ref, k_ref, v_ref):
    gains = [gain_ref[:, c * 128 : (c + 1) * 128] for c in range(4)]
    for r in range(4):
        rows = slice(r * 256, (r + 1) * 256)
        chunks = [x_ref[c * ROWS + r * 256 : c * ROWS + (r + 1) * 256, :].astype(F32) for c in range(4)]
        for c, part in enumerate(normed_chunks(chunks, gains)):
            normed[rows, c * 128 : (c + 1) * 128] = part
    everything = normed[...]
    q_ref[...] = (matmul(everything, w_ref[0]).astype(BF16).astype(F32) * 0.25).astype(BF16)
    k_ref[...] = matmul(everything, w_ref[1]).astype(BF16)
    v_ref[...] = matmul(everything, w_ref[2]).T.astype(BF16)
    head_of = lax.broadcasted_iota(jnp.int32, (STEP, LANES), 1) // HEAD_DIM
    work = [(h, part) for h in range(HEADS_HERE) for part in range(ROWS // STEP)]

    def scores_of(h, part):
        query = q_ref[part * STEP : (part + 1) * STEP, :].astype(F32)
        query = jnp.where(head_of == h, query, 0.0).astype(BF16)
        return matmul_nt(k_ref[...], query)

    scores = scores_of(*work[0])
    for n, (h, part) in enumerate(work):
        following = scores_of(*work[n + 1]) if n + 1 < len(work) else None
        top = jnp.max(scores, axis=0, keepdims=True)
        grown = jnp.exp(scores - top)
        share = 1.0 / jnp.sum(grown, axis=0, keepdims=True)
        probs = (grown * share).astype(BF16)
        result = matmul(v_ref[h * HEAD_DIM : (h + 1) * HEAD_DIM, :], probs).astype(BF16)
        for u in range(STEP // QUARTER):
            row = (part * (STEP // QUARTER) + u) * LANES + h * HEAD_DIM
            out_ref[row : row + HEAD_DIM, :] = result[:, u * QUARTER : (u + 1) * QUARTER]
        scores = following


def mlp_kernel(
    attn_ref, x_ref, gain_ref, cell_ref, mine_ref, other_ref, square_ref,
    block_ref, own_ref, swap_ref, next_ref,
):
    chan = lax.axis_index("chan")
    me = lax.axis_index("pts")
    core = lax.rem(me, 2)
    row = pl.multiple_of(chan * QUARTER, QUARTER)

    def columns(ref, base, height, count):
        return jnp.concatenate([ref[base + r * height : base + (r + 1) * height, :] for r in range(count)], axis=1)

    def stacked(parts):
        return jnp.concatenate(parts, axis=0)

    x = jnp.concatenate([x_ref[pl.ds(c * ROWS + row, QUARTER), :] for c in range(4)], axis=1)
    w_out = stacked([columns(square_ref, c * SQUARE_ROWS, 128, 4) for c in range(4)])
    mid = (x.astype(F32) + matmul_tn(attn_ref[...], w_out)).astype(BF16).astype(F32)
    normed = normed_chunks([mid], [gain_ref[...]])[0]
    summed = None
    for ref in (mine_ref, other_ref):
        for c in range(0, 4, 2):
            bases = (c * HALF_ROWS, (c + 1) * HALF_ROWS)
            w_fc1 = jnp.concatenate([columns(ref, base, C, 2) for base in bases], axis=1)
            w_fc2 = stacked([columns(ref, base + 2 * C, HALF, 4) for base in bases])
            act = gelu(matmul(normed, w_fc1)).astype(BF16)
            term = matmul(act, w_fc2)
            summed = term if summed is None else summed + term
    block = (mid + summed).astype(BF16)
    w_pool = jnp.concatenate([square_ref[c * SQUARE_ROWS + C : (c + 1) * SQUARE_ROWS, :] for c in range(4)], axis=1)
    lin = matmul(block, w_pool)
    high = lin.astype(BF16)
    low = (lin - high.astype(F32)).astype(BF16)
    member = one_hot(cell_ref[:, pl.ds(row, QUARTER)] - (me - 1) * CELLS, 3 * CELLS)
    sums = matmul(member, high) + matmul(member, low)
    block_ref[...] = block
    own_ref[...] = sums[CELLS : 2 * CELLS]
    before = sums[:CELLS].astype(BF16)
    after = sums[2 * CELLS :].astype(BF16)

    @pl.when(core == 0)
    def _():
        swap_ref[...] = after
        next_ref[...] = before

    @pl.when(core == 1)
    def _():
        swap_ref[...] = before
        next_ref[...] = after


def message_kernel(block_ref, own_ref, swap_ref, next_ref, out_ref):
    sums = own_ref[...] + swap_ref[...].astype(F32) + next_ref[...].astype(F32)
    sums = sums.astype(BF16)
    for c in range(N_CHAN):
        cols = slice(c * 128, (c + 1) * 128)
        out_ref[c * MESSAGE : c * MESSAGE + QUARTER, :] = block_ref[:, cols]
        out_ref[c * MESSAGE + QUARTER : (c + 1) * MESSAGE, :] = sums[:, cols]


def pool_kernel(got_ref, count_ref, block_ref, out_ref):
    total = jnp.zeros((CELLS, LANES), F32)
    for c in range(N_CHAN):
        block_ref[c * QUARTER : (c + 1) * QUARTER, :] = got_ref[c * MESSAGE : c * MESSAGE + QUARTER, :]
        total = total + got_ref[c * MESSAGE + QUARTER : (c + 1) * MESSAGE, :].astype(F32)
    out_ref[...] = gelu(total / count_ref[...]).astype(BF16)


def call(kernel, outs, args, scratch=(), in_hbm=(), out_hbm=(), limit=VMEM_LIMIT):
    vmem = pl.BlockSpec(memory_space=pltpu.VMEM)
    hbm = pl.BlockSpec(memory_space=pltpu.HBM)
    return pl.pallas_call(
        kernel,
        out_shape=[jax.ShapeDtypeStruct(shape, dtype) for shape, dtype in outs],
        in_specs=[hbm if i in in_hbm else vmem for i in range(len(args))],
        out_specs=[hbm if i in out_hbm else vmem for i in range(len(outs))],
        scratch_shapes=list(scratch),
        compiler_params=pltpu.CompilerParams(vmem_limit_bytes=limit),
    )(*args)


def body(feats, dest_pos, cell_id, ln1_gain, w_qkv, w_out, ln2_gain, w_fc1, w_fc2, w_pool):
    def block(count=1):
        return ((count * BLOCK, LANES), BF16)

    up, down, swap, far, over, halves, square = call(
        pack_kernel,
        [block(2), block(2), block(2), block(), block(), ((HALF_ROWS, LANES), BF16), ((SQUARE_ROWS, LANES), BF16)],
        (feats, dest_pos.reshape(1, ROWS), cell_id.reshape(1, ROWS), w_out, w_fc1, w_fc2, w_pool),
        scratch=[
            pltpu.VMEM((ROWS, LANES), BF16),
            pltpu.VMEM((1, ROWS), jnp.int32),
            pltpu.VMEM((1, ROWS), jnp.int32),
            pltpu.SemaphoreType.DMA((14,)),
        ],
        limit=ALL_VMEM,
        in_hbm=range(7),
    )
    halves = lax.all_gather(halves, "chan", axis=0, tiled=True)
    far = exchange(far, far_pair)
    over = exchange(over, across)
    up = exchange(up, chip_up)
    down = exchange(down, chip_down)
    swap, far, over = lax.optimization_barrier((swap, far, over))
    sent = jnp.concatenate([swap, up[BLOCK:], down[BLOCK:]], axis=0)
    swap = exchange(sent, core_swap)
    ordered, count = call(
        unpack_kernel,
        [((N_CHAN * ROWS, LANES), BF16), ((128, 128), F32)],
        (sent, up, down, far, over, swap),
        scratch=[pltpu.VMEM((SLOTS, LANES), BF16)],
    )
    full = lax.all_to_all(ordered, "chan", split_axis=0, concat_axis=0, tiled=True)
    full, square, halves = lax.optimization_barrier((full, square, halves))
    square = lax.all_gather(square, "chan", axis=0, tiled=True)
    others = exchange(halves, core_swap)
    (attn,) = call(
        attention_kernel,
        [((N_CHAN * LANES, QUARTER), BF16)],
        (full, ln1_gain.reshape(1, C), w_qkv),
        scratch=[
            pltpu.VMEM((ROWS, C), BF16),
            pltpu.VMEM((ROWS, LANES), BF16),
            pltpu.VMEM((ROWS, LANES), BF16),
            pltpu.VMEM((LANES, ROWS), BF16),
        ],
    )
    attn = lax.all_to_all(attn, "chan", split_axis=0, concat_axis=0, tiled=True)
    cell_sum = ((CELLS, C), BF16)
    rows, mine, for_swap, for_next = call(
        mlp_kernel,
        [((QUARTER, C), BF16), ((CELLS, C), F32), cell_sum, cell_sum],
        (attn, full, ln2_gain.reshape(1, C), cell_id.reshape(1, ROWS), halves, others, square),
        limit=SOME_VMEM,
    )
    from_swap = exchange(for_swap, core_swap)
    from_next = exchange(for_next, next_pair)
    (message,) = call(
        message_kernel,
        [((N_CHAN * MESSAGE, LANES), BF16)],
        (rows, mine, from_swap, from_next),
    )
    got = lax.all_to_all(message, "chan", split_axis=0, concat_axis=0, tiled=True)
    block_out, pooled = call(
        pool_kernel, [((ROWS, LANES), BF16), ((CELLS, LANES), BF16)], (got, count)
    )
    return (block_out, pooled)


def solution(mesh):
    return jax.shard_map(
        body,
        mesh=mesh,
        in_specs=(
            P("pts", "chan"),
            P("pts"),
            P("pts"),
            P(),
            P(None, None, "chan"),
            P("chan", None),
            P(),
            P(None, "chan"),
            P("chan", None),
            P(None, "chan"),
        ),
        out_specs=(P("pts", "chan"), P("pts", "chan")),
        check_vma=False,
    )
```

```python
import jax
import jax.numpy as jnp
from jax import lax
from jax.experimental import pallas as pl
from jax.experimental.pallas import tpu as pltpu
from jax.sharding import PartitionSpec as P

F32 = jnp.float32
BF16 = jnp.bfloat16

N_PTS = 128
N_CHAN = 4
ROWS = 1024
C = 512
LANES = 128
HEADS_HERE = 8
HEAD_DIM = 16
QUARTER = ROWS // N_CHAN
CELLS = ROWS // 8
CAP = 192
BLOCK = CAP + 16
KINDS = 8
SLOTS = KINDS * CAP
HALF = 256
STEP = 512
FC1, FC2, POOL, WROWS = 256, 1280, 2304, 2560
MESSAGE = QUARTER + CELLS
VMEM_LIMIT = 32 * 1024 * 1024
SOME_VMEM = 32 * 1024 * 1024
ALL_VMEM = 63 * 1024 * 1024 + 512 * 1024


def chip_up(i):
    return (i + 2 if (i >> 1) % 2 == 0 else i - 2) % N_PTS


def chip_down(i):
    return (i - 2 if (i >> 1) % 2 == 0 else i + 2) % N_PTS


def core_swap(i):
    return i ^ 1


def next_pair(i):
    return (i - 1 if i % 2 == 0 else i + 1) % N_PTS


def far_pair(i):
    return (i - 3 if i % 2 == 0 else i + 3) % N_PTS


def across(i):
    return (i + N_PTS // 2) % N_PTS


def exchange(x, partner):
    return lax.ppermute(x, "pts", [(i, partner(i)) for i in range(N_PTS)])


def offsets_of(me):
    core = lax.rem(me, 2)
    chip = lax.rem(me // 2, 2)
    up = 2 - 4 * chip
    swap = 1 - 2 * core
    return [0 * me, up, up + swap, -up, swap - up, swap, 6 * core - 3, 0 * me + 64]


def matmul(a, b):
    return jnp.dot(a, b, preferred_element_type=F32)


def matmul_nt(a, b):
    return lax.dot_general(a, b, (((1,), (1,)), ((), ())), preferred_element_type=F32)


def matmul_tn(a, b):
    return lax.dot_general(a, b, (((0,), (0,)), ((), ())), preferred_element_type=F32)


def one_hot(row, height):
    index = lax.broadcasted_iota(jnp.int32, (height, row.shape[1]), 0)
    return jnp.where(index == row, 1.0, 0.0).astype(BF16)


def gelu(x):
    return 0.5 * x * (1.0 + lax.erf(x * 0.7071067811865476))


def normed_chunks(chunks, gains):
    total = chunks[0]
    for x in chunks[1:]:
        total = total + x
    mean = jnp.sum(total, axis=-1, keepdims=True) * (1.0 / C)
    centered = [x - mean for x in chunks]
    square = centered[0] * centered[0]
    for x in centered[1:]:
        square = square + x * x
    var = jnp.sum(square, axis=-1, keepdims=True) * (1.0 / C)
    scale = lax.rsqrt(var + 1e-05)
    return [(x * scale * g).astype(BF16) for x, g in zip(centered, gains)]


def copier(sems):
    copies = []

    def start(src, dst):
        copy = pltpu.make_async_copy(src, dst, sems.at[len(copies)])
        copy.start()
        copies.append(copy)
        return copy

    return start


def wait(copies):
    for copy in copies:
        copy.wait()


def digits_of(dest):
    local = dest & (ROWS - 1)
    line = lax.broadcasted_iota(jnp.int32, (16, ROWS), 0)
    digits = jnp.where(line == 0, (local >> 5) + 1, jnp.where(line == 1, local & 31, 0))
    return digits.astype(F32).astype(BF16)


def cell_counts(cell, me):
    relative = cell - (me - 1) * CELLS
    counts = matmul_nt(jnp.full((16, ROWS), 1.0, BF16), one_hot(relative, 3 * CELLS))
    return counts[0:1, :].astype(jnp.int32)


def write_blocks(slot, dest, feats, blocks, counts):
    small = lax.broadcasted_iota(jnp.int32, (16, 128), 0)
    lane = lax.broadcasted_iota(jnp.int32, (1, 128), 1)
    chosen = one_hot(slot, SLOTS)
    packed = matmul(chosen, feats).astype(BF16)
    places = matmul_nt(digits_of(dest), chosen)
    for m, (ref, base, offset) in enumerate(blocks):
        ref[base : base + 128, :] = packed[m * 128 : (m + 1) * 128, :]
        ref[base + 128 : base + CAP, :] = packed[1024 + m * 64 : 1024 + (m + 1) * 64, :]
        first = places[0:2, m * 128 : (m + 1) * 128]
        mine = (lane >= 64) if m % 2 else (lane < 64)
        tile = 1024 + (m // 2) * 128
        second = jnp.where(mine, places[0:2, tile : tile + 128], 0.0)
        count = jnp.zeros((1, CELLS), jnp.int32)
        for away in (-1, 0, 1):
            near = jnp.where(offset == away, 1, 0)
            count = count + counts[:, (away + 1) * CELLS : (away + 2) * CELLS] * near
        rows = [
            first[0:1], first[1:2], second[0:1], second[1:2],
            (count >> 5).astype(F32), (count & 31).astype(F32),
        ]
        notes = jnp.zeros((16, 128), F32)
        for r, value in enumerate(rows):
            notes = jnp.where(small == r, value, notes)
        ref[base + CAP : base + BLOCK, :] = notes.astype(BF16)


def pack_kernel(
    feats_ref, dest_ref, cell_ref, w_out_ref, w_fc1_ref, w_fc2_ref, w_pool_ref,
    up_ref, down_ref, swap_ref, far_ref, across_ref, weights_ref,
    feats_here, dest_here, cell_here, sems,
):
    me = lax.axis_index("pts")
    core = lax.rem(me, 2)
    start = copier(sems)
    dest_copy = start(dest_ref, dest_here)
    cell_copy = start(cell_ref, cell_here)
    feats_copy = start(feats_ref, feats_here)

    half = pl.multiple_of(core * HALF, HALF)
    quarter = pl.multiple_of(core * 64, 64)
    weight_copies = []
    for r in range(2):
        src = w_fc1_ref.at[:, pl.ds(pl.multiple_of(half + r * 128, 128), 128)]
        weight_copies.append(start(src, weights_ref.at[FC1 + r * C : FC1 + (r + 1) * C, :]))
    for r in range(4):
        cols = slice(r * 128, (r + 1) * 128)
        dst = weights_ref.at[FC2 + r * HALF : FC2 + (r + 1) * HALF, :]
        weight_copies.append(start(w_fc2_ref.at[pl.ds(half, HALF), cols], dst))
        dst = weights_ref.at[r * 64 : (r + 1) * 64, :]
        weight_copies.append(start(w_out_ref.at[pl.ds(quarter, 64), cols], dst))
    weight_copies.append(start(w_pool_ref.at[pl.ds(half, HALF), :], weights_ref.at[POOL:WROWS, :]))

    before = lax.broadcasted_iota(jnp.int32, (ROWS, ROWS), 0)
    after = lax.broadcasted_iota(jnp.int32, (ROWS, ROWS), 1)
    earlier = jnp.where(before < after, 1.0, 0.0).astype(BF16)
    wait([dest_copy])
    offsets = offsets_of(me)
    dest = dest_here[...]
    away = ((dest >> 10) - me) & (N_PTS - 1)
    kind = jnp.zeros_like(dest)
    for m in range(1, KINDS):
        kind = jnp.where(away == (offsets[m] & (N_PTS - 1)), m, kind)

    kinds = one_hot(kind, 16)
    ranks = matmul(kinds, earlier) * kinds.astype(F32)
    rank = jnp.sum(ranks, axis=0, keepdims=True).astype(jnp.int32)
    slot = jnp.where(rank < 128, kind * 128 + rank, 1024 - 128 + kind * 64 + rank)
    homes = [
        (swap_ref, BLOCK), (up_ref, 0), (up_ref, BLOCK), (down_ref, 0),
        (down_ref, BLOCK), (swap_ref, 0), (far_ref, 0), (across_ref, 0),
    ]
    blocks = [home + (offset,) for home, offset in zip(homes, offsets)]
    wait([cell_copy])
    counts = cell_counts(cell_here[...], me)
    wait([feats_copy])
    write_blocks(slot, dest, feats_here[...], blocks, counts)
    wait(weight_copies)


def unpack_kernel(sent_ref, down_ref, up_ref, across_ref, far_ref, swap_ref, out_ref, count_ref, held):
    homes = [
        (sent_ref, BLOCK), (up_ref, 0), (swap_ref, 2 * BLOCK), (down_ref, 0),
        (swap_ref, 3 * BLOCK), (swap_ref, 0), (far_ref, 0), (across_ref, 0),
    ]
    firsts, seconds = [], []
    count = jnp.zeros((1, 128), F32)
    for m, (ref, base) in enumerate(homes):
        held[m * 128 : (m + 1) * 128, :] = ref[base : base + 128, :]
        held[1024 + m * 64 : 1024 + (m + 1) * 64, :] = ref[base + 128 : base + CAP, :]
        notes = ref[base + CAP : base + BLOCK, :].astype(F32)
        firsts.append(notes[0:1] * 32.0 + notes[1:2] - 32.0)
        seconds.append(notes[2:3] * 32.0 + notes[3:4])
        count = count + notes[4:5] * 32.0 + notes[5:6]
    pairs = [seconds[m] + seconds[m + 1] - 32.0 for m in range(0, KINDS, 2)]
    places = jnp.concatenate(firsts + pairs, axis=1).astype(jnp.int32)
    ordered = matmul(one_hot(places, ROWS), held[...]).astype(BF16)
    for c in range(N_CHAN):
        out_ref[c * ROWS : (c + 1) * ROWS, :] = ordered
    count_ref[...] = jnp.broadcast_to(count, (128, 128)).T


def attention_kernel(x_ref, gain_ref, w_ref, out_ref, normed, q_ref, k_ref, v_ref):
    gains = [gain_ref[:, c * 128 : (c + 1) * 128] for c in range(4)]
    for r in range(4):
        rows = slice(r * 256, (r + 1) * 256)
        chunks = [x_ref[c * ROWS + r * 256 : c * ROWS + (r + 1) * 256, :].astype(F32) for c in range(4)]
        for c, part in enumerate(normed_chunks(chunks, gains)):
            normed[rows, c * 128 : (c + 1) * 128] = part
    everything = normed[...]
    q_ref[...] = (matmul(everything, w_ref[0]).astype(BF16).astype(F32) * 0.25).astype(BF16)
    k_ref[...] = matmul(everything, w_ref[1]).astype(BF16)
    v_ref[...] = matmul(everything, w_ref[2]).T.astype(BF16)
    head_of = lax.broadcasted_iota(jnp.int32, (STEP, LANES), 1) // HEAD_DIM
    work = [(h, part) for h in range(HEADS_HERE) for part in range(ROWS // STEP)]

    def scores_of(h, part):
        query = q_ref[part * STEP : (part + 1) * STEP, :].astype(F32)
        query = jnp.where(head_of == h, query, 0.0).astype(BF16)
        return matmul_nt(k_ref[...], query)

    scores = scores_of(*work[0])
    for n, (h, part) in enumerate(work):
        following = scores_of(*work[n + 1]) if n + 1 < len(work) else None
        top = jnp.max(scores, axis=0, keepdims=True)
        grown = jnp.exp(scores - top)
        share = 1.0 / jnp.sum(grown, axis=0, keepdims=True)
        probs = (grown * share).astype(BF16)
        result = matmul(v_ref[h * HEAD_DIM : (h + 1) * HEAD_DIM, :], probs).astype(BF16)
        for u in range(STEP // QUARTER):
            row = (part * (STEP // QUARTER) + u) * LANES + h * HEAD_DIM
            out_ref[row : row + HEAD_DIM, :] = result[:, u * QUARTER : (u + 1) * QUARTER]
        scores = following


def mlp_kernel(
    attn_ref, x_ref, gain_ref, cell_ref, mine_ref, other_ref,
    block_ref, own_ref, swap_ref, next_ref,
):
    chan = lax.axis_index("chan")
    me = lax.axis_index("pts")
    core = lax.rem(me, 2)
    row = pl.multiple_of(chan * QUARTER, QUARTER)

    def columns(ref, base, height, count):
        return jnp.concatenate([ref[base + r * height : base + (r + 1) * height, :] for r in range(count)], axis=1)

    def stacked(parts):
        return jnp.concatenate(parts, axis=0)

    x = jnp.concatenate([x_ref[pl.ds(c * ROWS + row, QUARTER), :] for c in range(4)], axis=1)
    halves = ((core, mine_ref), (1 - core, other_ref))
    rows, w_out = [], []
    for which, ref in halves:
        for c in range(4):
            rows.append(attn_ref[pl.ds(pl.multiple_of(c * 128 + which * 64, 64), 64), :])
            w_out.append(columns(ref, c * WROWS, 64, 4))
    mid = (x.astype(F32) + matmul_tn(stacked(rows), stacked(w_out))).astype(BF16).astype(F32)
    normed = normed_chunks([mid], [gain_ref[...]])[0]
    summed = None
    for _, ref in halves:
        for c in range(0, 4, 2):
            bases = (c * WROWS, (c + 1) * WROWS)
            w_fc1 = jnp.concatenate([columns(ref, base + FC1, C, 2) for base in bases], axis=1)
            w_fc2 = stacked([columns(ref, base + FC2, HALF, 4) for base in bases])
            act = gelu(matmul(normed, w_fc1)).astype(BF16)
            term = matmul(act, w_fc2)
            summed = term if summed is None else summed + term
    block = (mid + summed).astype(BF16)
    left, right = block[:, :HALF].astype(F32), block[:, HALF:].astype(F32)
    lin = None
    for which, ref in halves:
        mine = jnp.where(which == 0, left, right).astype(BF16)
        w_pool = jnp.concatenate([ref[c * WROWS + POOL : (c + 1) * WROWS, :] for c in range(4)], axis=1)
        term = matmul(mine, w_pool)
        lin = term if lin is None else lin + term
    high = lin.astype(BF16)
    low = (lin - high.astype(F32)).astype(BF16)
    member = one_hot(cell_ref[:, pl.ds(row, QUARTER)] - (me - 1) * CELLS, 3 * CELLS)
    sums = matmul(member, high) + matmul(member, low)
    block_ref[...] = block
    own_ref[...] = sums[CELLS : 2 * CELLS]
    before = sums[:CELLS].astype(BF16)
    after = sums[2 * CELLS :].astype(BF16)

    @pl.when(core == 0)
    def _():
        swap_ref[...] = after
        next_ref[...] = before

    @pl.when(core == 1)
    def _():
        swap_ref[...] = before
        next_ref[...] = after


def message_kernel(block_ref, own_ref, next_ref, swap_ref, out_ref):
    sums = own_ref[...] + swap_ref[...].astype(F32) + next_ref[...].astype(F32)
    sums = sums.astype(BF16)
    for c in range(N_CHAN):
        cols = slice(c * 128, (c + 1) * 128)
        out_ref[c * MESSAGE : c * MESSAGE + QUARTER, :] = block_ref[:, cols]
        out_ref[c * MESSAGE + QUARTER : (c + 1) * MESSAGE, :] = sums[:, cols]


def pool_kernel(got_ref, count_ref, block_ref, out_ref):
    total = jnp.zeros((CELLS, LANES), F32)
    for c in range(N_CHAN):
        block_ref[c * QUARTER : (c + 1) * QUARTER, :] = got_ref[c * MESSAGE : c * MESSAGE + QUARTER, :]
        total = total + got_ref[c * MESSAGE + QUARTER : (c + 1) * MESSAGE, :].astype(F32)
    out_ref[...] = gelu(total / count_ref[...]).astype(BF16)


def call(kernel, outs, args, scratch=(), in_hbm=(), limit=VMEM_LIMIT, cost=None):
    vmem = pl.BlockSpec(memory_space=pltpu.VMEM)
    hbm = pl.BlockSpec(memory_space=pltpu.HBM)
    return pl.pallas_call(
        kernel,
        out_shape=[jax.ShapeDtypeStruct(shape, dtype) for shape, dtype in outs],
        in_specs=[hbm if i in in_hbm else vmem for i in range(len(args))],
        out_specs=[vmem] * len(outs),
        scratch_shapes=list(scratch),
        compiler_params=pltpu.CompilerParams(vmem_limit_bytes=limit),
        cost_estimate=cost,
    )(*args)


def body(feats, dest_pos, cell_id, ln1_gain, w_qkv, w_out, ln2_gain, w_fc1, w_fc2, w_pool):
    def block(count=1):
        return ((count * BLOCK, LANES), BF16)

    up, down, swap, far, over, weights = call(
        pack_kernel,
        [block(2), block(2), block(2), block(), block(), ((WROWS, LANES), BF16)],
        (feats, dest_pos.reshape(1, ROWS), cell_id.reshape(1, ROWS), w_out, w_fc1, w_fc2, w_pool),
        scratch=[
            pltpu.VMEM((ROWS, LANES), BF16),
            pltpu.VMEM((1, ROWS), jnp.int32),
            pltpu.VMEM((1, ROWS), jnp.int32),
            pltpu.SemaphoreType.DMA((14,)),
        ],
        limit=ALL_VMEM,
        in_hbm=range(7),
    )
    weights = lax.all_gather(weights, "chan", axis=0, tiled=True)
    down = exchange(down, chip_down)
    up = exchange(up, chip_up)
    over = exchange(over, across)
    far = exchange(far, far_pair)
    swap, over, far = lax.optimization_barrier((swap, over, far))
    sent = jnp.concatenate([swap, up[BLOCK:], down[BLOCK:]], axis=0)
    swap = exchange(sent, core_swap)
    ordered, count = call(
        unpack_kernel,
        [((N_CHAN * ROWS, LANES), BF16), ((128, 128), F32)],
        (sent, down, up, over, far, swap),
        scratch=[pltpu.VMEM((SLOTS, LANES), BF16)],
    )
    full = lax.all_to_all(ordered, "chan", split_axis=0, concat_axis=0, tiled=True)
    full, weights = lax.optimization_barrier((full, weights))
    others = exchange(weights, core_swap)
    (attn,) = call(
        attention_kernel,
        [((N_CHAN * LANES, QUARTER), BF16)],
        (full, ln1_gain.reshape(1, C), w_qkv),
        cost=pl.CostEstimate(flops=9_000_000_000, bytes_accessed=2_000_000, transcendentals=8_400_000),
        scratch=[
            pltpu.VMEM((ROWS, C), BF16),
            pltpu.VMEM((ROWS, LANES), BF16),
            pltpu.VMEM((ROWS, LANES), BF16),
            pltpu.VMEM((LANES, ROWS), BF16),
        ],
    )
    attn = lax.all_to_all(attn, "chan", split_axis=0, concat_axis=0, tiled=True)
    cell_sum = ((CELLS, C), BF16)
    rows, mine, for_swap, for_next = call(
        mlp_kernel,
        [((QUARTER, C), BF16), ((CELLS, C), F32), cell_sum, cell_sum],
        (attn, full, ln2_gain.reshape(1, C), cell_id.reshape(1, ROWS), weights, others),
        limit=SOME_VMEM,
    )
    from_next = exchange(for_next, next_pair)
    from_swap = exchange(for_swap, core_swap)
    (message,) = call(
        message_kernel,
        [((N_CHAN * MESSAGE, LANES), BF16)],
        (rows, mine, from_next, from_swap),
    )
    got = lax.all_to_all(message, "chan", split_axis=0, concat_axis=0, tiled=True)
    block_out, pooled = call(
        pool_kernel, [((ROWS, LANES), BF16), ((CELLS, LANES), BF16)], (got, count)
    )
    return (block_out, pooled)


def solution(mesh):
    return jax.shard_map(
        body,
        mesh=mesh,
        in_specs=(
            P("pts", "chan"),
            P("pts"),
            P("pts"),
            P(),
            P(None, None, "chan"),
            P("chan", None),
            P(),
            P(None, "chan"),
            P("chan", None),
            P(None, "chan"),
        ),
        out_specs=(P("pts", "chan"), P("pts", "chan")),
        check_vma=False,
    )
```

```python
import jax
import jax.numpy as jnp
from jax import lax
from jax.experimental import pallas as pl
from jax.experimental.pallas import tpu as pltpu
from jax.sharding import PartitionSpec as P

F32 = jnp.float32
BF16 = jnp.bfloat16

N_PTS = 128
N_CHAN = 4
ROWS = 1024
C = 512
LANES = 128
HEADS_HERE = 8
HEAD_DIM = 16
QUARTER = ROWS // N_CHAN
CELLS = ROWS // 8
CAP = 192
BLOCK = CAP + 16
KINDS = 8
SLOTS = KINDS * CAP
HALF = 256
STEP = 512
FC1, FC2, POOL, WROWS = 256, 1280, 2304, 2560
MESSAGE = QUARTER + CELLS
VMEM_LIMIT = 32 * 1024 * 1024
SOME_VMEM = 32 * 1024 * 1024
ALL_VMEM = 63 * 1024 * 1024 + 512 * 1024


def chip_up(i):
    return (i + 2 if (i >> 1) % 2 == 0 else i - 2) % N_PTS


def chip_down(i):
    return (i - 2 if (i >> 1) % 2 == 0 else i + 2) % N_PTS


def core_swap(i):
    return i ^ 1


def next_pair(i):
    return (i - 1 if i % 2 == 0 else i + 1) % N_PTS


def far_pair(i):
    return (i - 3 if i % 2 == 0 else i + 3) % N_PTS


def across(i):
    return (i + N_PTS // 2) % N_PTS


def exchange(x, partner):
    return lax.ppermute(x, "pts", [(i, partner(i)) for i in range(N_PTS)])


def offsets_of(me):
    core = lax.rem(me, 2)
    chip = lax.rem(me // 2, 2)
    up = 2 - 4 * chip
    swap = 1 - 2 * core
    return [0 * me, up, up + swap, -up, swap - up, swap, 6 * core - 3, 0 * me + 64]


def matmul(a, b):
    return jnp.dot(a, b, preferred_element_type=F32)


def matmul_nt(a, b):
    return lax.dot_general(a, b, (((1,), (1,)), ((), ())), preferred_element_type=F32)


def matmul_tn(a, b):
    return lax.dot_general(a, b, (((0,), (0,)), ((), ())), preferred_element_type=F32)


def one_hot(row, height):
    index = lax.broadcasted_iota(jnp.int32, (height, row.shape[1]), 0)
    return jnp.where(index == row, 1.0, 0.0).astype(BF16)


def gelu(x):
    return 0.5 * x * (1.0 + lax.erf(x * 0.7071067811865476))


def normed_chunks(chunks, gains):
    total = chunks[0]
    for x in chunks[1:]:
        total = total + x
    mean = jnp.sum(total, axis=-1, keepdims=True) * (1.0 / C)
    centered = [x - mean for x in chunks]
    square = centered[0] * centered[0]
    for x in centered[1:]:
        square = square + x * x
    var = jnp.sum(square, axis=-1, keepdims=True) * (1.0 / C)
    scale = lax.rsqrt(var + 1e-05)
    return [(x * scale * g).astype(BF16) for x, g in zip(centered, gains)]


def copier(sems):
    copies = []

    def start(src, dst):
        copy = pltpu.make_async_copy(src, dst, sems.at[len(copies)])
        copy.start()
        copies.append(copy)
        return copy

    return start


def wait(copies):
    for copy in copies:
        copy.wait()


def digits_of(dest):
    local = dest & (ROWS - 1)
    line = lax.broadcasted_iota(jnp.int32, (16, ROWS), 0)
    digits = jnp.where(line == 0, (local >> 5) + 1, jnp.where(line == 1, local & 31, 0))
    return digits.astype(F32).astype(BF16)


def cell_counts(cell, me):
    relative = cell - (me - 1) * CELLS
    counts = matmul_nt(jnp.full((16, ROWS), 1.0, BF16), one_hot(relative, 3 * CELLS))
    return counts[0:1, :].astype(jnp.int32)


def write_blocks(slot, dest, feats, blocks, counts):
    small = lax.broadcasted_iota(jnp.int32, (16, 128), 0)
    lane = lax.broadcasted_iota(jnp.int32, (1, 128), 1)
    chosen = one_hot(slot, SLOTS)
    packed = matmul(chosen, feats).astype(BF16)
    places = matmul_nt(digits_of(dest), chosen)
    for m, (ref, base, offset) in enumerate(blocks):
        ref[base : base + 128, :] = packed[m * 128 : (m + 1) * 128, :]
        ref[base + 128 : base + CAP, :] = packed[1024 + m * 64 : 1024 + (m + 1) * 64, :]
        first = places[0:2, m * 128 : (m + 1) * 128]
        mine = (lane >= 64) if m % 2 else (lane < 64)
        tile = 1024 + (m // 2) * 128
        second = jnp.where(mine, places[0:2, tile : tile + 128], 0.0)
        count = jnp.zeros((1, CELLS), jnp.int32)
        for away in (-1, 0, 1):
            near = jnp.where(offset == away, 1, 0)
            count = count + counts[:, (away + 1) * CELLS : (away + 2) * CELLS] * near
        rows = [
            first[0:1], first[1:2], second[0:1], second[1:2],
            (count >> 5).astype(F32), (count & 31).astype(F32),
        ]
        notes = jnp.zeros((16, 128), F32)
        for r, value in enumerate(rows):
            notes = jnp.where(small == r, value, notes)
        ref[base + CAP : base + BLOCK, :] = notes.astype(BF16)


def weights_kernel(w_out_ref, w_fc1_ref, w_fc2_ref, w_pool_ref, out_ref, sems):
    core = lax.rem(lax.axis_index("pts"), 2)
    start = copier(sems)
    half = pl.multiple_of(core * HALF, HALF)
    quarter = pl.multiple_of(core * 64, 64)
    copies = []
    for r in range(2):
        src = w_fc1_ref.at[:, pl.ds(pl.multiple_of(half + r * 128, 128), 128)]
        copies.append(start(src, out_ref.at[FC1 + r * C : FC1 + (r + 1) * C, :]))
    for r in range(4):
        cols = slice(r * 128, (r + 1) * 128)
        dst = out_ref.at[FC2 + r * HALF : FC2 + (r + 1) * HALF, :]
        copies.append(start(w_fc2_ref.at[pl.ds(half, HALF), cols], dst))
        dst = out_ref.at[r * 64 : (r + 1) * 64, :]
        copies.append(start(w_out_ref.at[pl.ds(quarter, 64), cols], dst))
    copies.append(start(w_pool_ref.at[pl.ds(half, HALF), :], out_ref.at[POOL:WROWS, :]))
    wait(copies)


def pack_kernel(
    feats_ref, dest_ref, cell_ref, up_ref, down_ref, swap_ref, far_ref, across_ref,
    feats_here, dest_here, cell_here, sems,
):
    me = lax.axis_index("pts")
    start = copier(sems)
    dest_copy = start(dest_ref, dest_here)
    cell_copy = start(cell_ref, cell_here)
    feats_copy = start(feats_ref, feats_here)
    before = lax.broadcasted_iota(jnp.int32, (ROWS, ROWS), 0)
    after = lax.broadcasted_iota(jnp.int32, (ROWS, ROWS), 1)
    earlier = jnp.where(before < after, 1.0, 0.0).astype(BF16)
    wait([dest_copy])
    offsets = offsets_of(me)
    dest = dest_here[...]
    away = ((dest >> 10) - me) & (N_PTS - 1)
    kind = jnp.zeros_like(dest)
    for m in range(1, KINDS):
        kind = jnp.where(away == (offsets[m] & (N_PTS - 1)), m, kind)

    kinds = one_hot(kind, 16)
    ranks = matmul(kinds, earlier) * kinds.astype(F32)
    rank = jnp.sum(ranks, axis=0, keepdims=True).astype(jnp.int32)
    slot = jnp.where(rank < 128, kind * 128 + rank, 1024 - 128 + kind * 64 + rank)
    homes = [
        (swap_ref, BLOCK), (up_ref, 0), (up_ref, BLOCK), (down_ref, 0),
        (down_ref, BLOCK), (swap_ref, 0), (far_ref, 0), (across_ref, 0),
    ]
    blocks = [home + (offset,) for home, offset in zip(homes, offsets)]
    wait([cell_copy])
    counts = cell_counts(cell_here[...], me)
    wait([feats_copy])
    write_blocks(slot, dest, feats_here[...], blocks, counts)


def unpack_kernel(sent_ref, down_ref, up_ref, across_ref, far_ref, swap_ref, out_ref, count_ref, held):
    homes = [
        (sent_ref, BLOCK), (up_ref, 0), (swap_ref, 2 * BLOCK), (down_ref, 0),
        (swap_ref, 3 * BLOCK), (swap_ref, 0), (far_ref, 0), (across_ref, 0),
    ]
    firsts, seconds = [], []
    count = jnp.zeros((1, 128), F32)
    for m, (ref, base) in enumerate(homes):
        held[m * 128 : (m + 1) * 128, :] = ref[base : base + 128, :]
        held[1024 + m * 64 : 1024 + (m + 1) * 64, :] = ref[base + 128 : base + CAP, :]
        notes = ref[base + CAP : base + BLOCK, :].astype(F32)
        firsts.append(notes[0:1] * 32.0 + notes[1:2] - 32.0)
        seconds.append(notes[2:3] * 32.0 + notes[3:4])
        count = count + notes[4:5] * 32.0 + notes[5:6]
    pairs = [seconds[m] + seconds[m + 1] - 32.0 for m in range(0, KINDS, 2)]
    places = jnp.concatenate(firsts + pairs, axis=1).astype(jnp.int32)
    ordered = matmul(one_hot(places, ROWS), held[...]).astype(BF16)
    for c in range(N_CHAN):
        out_ref[c * ROWS : (c + 1) * ROWS, :] = ordered
    count_ref[...] = jnp.broadcast_to(count, (128, 128)).T


def attention_kernel(x_ref, gain_ref, w_ref, out_ref, normed, q_ref, k_ref, v_ref):
    gains = [gain_ref[:, c * 128 : (c + 1) * 128] for c in range(4)]
    for r in range(4):
        rows = slice(r * 256, (r + 1) * 256)
        chunks = [x_ref[c * ROWS + r * 256 : c * ROWS + (r + 1) * 256, :].astype(F32) for c in range(4)]
        for c, part in enumerate(normed_chunks(chunks, gains)):
            normed[rows, c * 128 : (c + 1) * 128] = part
    everything = normed[...]
    q_ref[...] = (matmul(everything, w_ref[0]).astype(BF16).astype(F32) * 0.25).astype(BF16)
    k_ref[...] = matmul(everything, w_ref[1]).astype(BF16)
    v_ref[...] = matmul(everything, w_ref[2]).T.astype(BF16)
    head_of = lax.broadcasted_iota(jnp.int32, (STEP, LANES), 1) // HEAD_DIM
    work = [(h, part) for h in range(HEADS_HERE) for part in range(ROWS // STEP)]

    def scores_of(h, part):
        query = q_ref[part * STEP : (part + 1) * STEP, :].astype(F32)
        query = jnp.where(head_of == h, query, 0.0).astype(BF16)
        return matmul_nt(k_ref[...], query)

    scores = scores_of(*work[0])
    for n, (h, part) in enumerate(work):
        following = scores_of(*work[n + 1]) if n + 1 < len(work) else None
        top = jnp.max(scores, axis=0, keepdims=True)
        grown = jnp.exp(scores - top)
        share = 1.0 / jnp.sum(grown, axis=0, keepdims=True)
        probs = (grown * share).astype(BF16)
        result = matmul(v_ref[h * HEAD_DIM : (h + 1) * HEAD_DIM, :], probs).astype(BF16)
        for u in range(STEP // QUARTER):
            row = (part * (STEP // QUARTER) + u) * LANES + h * HEAD_DIM
            out_ref[row : row + HEAD_DIM, :] = result[:, u * QUARTER : (u + 1) * QUARTER]
        scores = following


def mlp_kernel(
    attn_ref, x_ref, gain_ref, cell_ref, mine_ref, other_ref,
    block_ref, own_ref, swap_ref, next_ref,
):
    chan = lax.axis_index("chan")
    me = lax.axis_index("pts")
    core = lax.rem(me, 2)
    row = pl.multiple_of(chan * QUARTER, QUARTER)

    def columns(ref, base, height, count):
        return jnp.concatenate([ref[base + r * height : base + (r + 1) * height, :] for r in range(count)], axis=1)

    def stacked(parts):
        return jnp.concatenate(parts, axis=0)

    x = jnp.concatenate([x_ref[pl.ds(c * ROWS + row, QUARTER), :] for c in range(4)], axis=1)
    halves = ((core, mine_ref), (1 - core, other_ref))
    rows, w_out = [], []
    for which, ref in halves:
        for c in range(4):
            rows.append(attn_ref[pl.ds(pl.multiple_of(c * 128 + which * 64, 64), 64), :])
            w_out.append(columns(ref, c * WROWS, 64, 4))
    mid = (x.astype(F32) + matmul_tn(stacked(rows), stacked(w_out))).astype(BF16).astype(F32)
    normed = normed_chunks([mid], [gain_ref[...]])[0]
    summed = None
    for _, ref in halves:
        for c in range(0, 4, 2):
            bases = (c * WROWS, (c + 1) * WROWS)
            w_fc1 = jnp.concatenate([columns(ref, base + FC1, C, 2) for base in bases], axis=1)
            w_fc2 = stacked([columns(ref, base + FC2, HALF, 4) for base in bases])
            act = gelu(matmul(normed, w_fc1)).astype(BF16)
            term = matmul(act, w_fc2)
            summed = term if summed is None else summed + term
    block = (mid + summed).astype(BF16)
    left, right = block[:, :HALF].astype(F32), block[:, HALF:].astype(F32)
    lin = None
    for which, ref in halves:
        mine = jnp.where(which == 0, left, right).astype(BF16)
        w_pool = jnp.concatenate([ref[c * WROWS + POOL : (c + 1) * WROWS, :] for c in range(4)], axis=1)
        term = matmul(mine, w_pool)
        lin = term if lin is None else lin + term
    high = lin.astype(BF16)
    low = (lin - high.astype(F32)).astype(BF16)
    member = one_hot(cell_ref[:, pl.ds(row, QUARTER)] - (me - 1) * CELLS, 3 * CELLS)
    sums = matmul(member, high) + matmul(member, low)
    block_ref[...] = block
    own_ref[...] = sums[CELLS : 2 * CELLS]
    before = sums[:CELLS].astype(BF16)
    after = sums[2 * CELLS :].astype(BF16)

    @pl.when(core == 0)
    def _():
        swap_ref[...] = after
        next_ref[...] = before

    @pl.when(core == 1)
    def _():
        swap_ref[...] = before
        next_ref[...] = after


def message_kernel(block_ref, own_ref, next_ref, swap_ref, out_ref):
    sums = own_ref[...] + swap_ref[...].astype(F32) + next_ref[...].astype(F32)
    sums = sums.astype(BF16)
    for c in range(N_CHAN):
        cols = slice(c * 128, (c + 1) * 128)
        out_ref[c * MESSAGE : c * MESSAGE + QUARTER, :] = block_ref[:, cols]
        out_ref[c * MESSAGE + QUARTER : (c + 1) * MESSAGE, :] = sums[:, cols]


def pool_kernel(got_ref, count_ref, block_ref, out_ref):
    total = jnp.zeros((CELLS, LANES), F32)
    for c in range(N_CHAN):
        block_ref[c * QUARTER : (c + 1) * QUARTER, :] = got_ref[c * MESSAGE : c * MESSAGE + QUARTER, :]
        total = total + got_ref[c * MESSAGE + QUARTER : (c + 1) * MESSAGE, :].astype(F32)
    out_ref[...] = gelu(total / count_ref[...]).astype(BF16)


def call(kernel, outs, args, scratch=(), in_hbm=(), limit=VMEM_LIMIT, cost=None):
    vmem = pl.BlockSpec(memory_space=pltpu.VMEM)
    hbm = pl.BlockSpec(memory_space=pltpu.HBM)
    return pl.pallas_call(
        kernel,
        out_shape=[jax.ShapeDtypeStruct(shape, dtype) for shape, dtype in outs],
        in_specs=[hbm if i in in_hbm else vmem for i in range(len(args))],
        out_specs=[vmem] * len(outs),
        scratch_shapes=list(scratch),
        compiler_params=pltpu.CompilerParams(vmem_limit_bytes=limit),
        cost_estimate=cost,
    )(*args)


def body(feats, dest_pos, cell_id, ln1_gain, w_qkv, w_out, ln2_gain, w_fc1, w_fc2, w_pool):
    def block(count=1):
        return ((count * BLOCK, LANES), BF16)

    (weights,) = call(
        weights_kernel,
        [((WROWS, LANES), BF16)],
        (w_out, w_fc1, w_fc2, w_pool),
        scratch=[pltpu.SemaphoreType.DMA((11,))],
        limit=ALL_VMEM,
        in_hbm=range(4),
    )
    weights = lax.all_gather(weights, "chan", axis=0, tiled=True)
    up, down, swap, far, over = call(
        pack_kernel,
        [block(2), block(2), block(2), block(), block()],
        (feats, dest_pos.reshape(1, ROWS), cell_id.reshape(1, ROWS)),
        scratch=[
            pltpu.VMEM((ROWS, LANES), BF16),
            pltpu.VMEM((1, ROWS), jnp.int32),
            pltpu.VMEM((1, ROWS), jnp.int32),
            pltpu.SemaphoreType.DMA((3,)),
        ],
        limit=ALL_VMEM,
        in_hbm=range(3),
    )
    far = exchange(far, far_pair)
    over = exchange(over, across)
    down = exchange(down, chip_down)
    up, far, over = lax.optimization_barrier((up, far, over))
    up = exchange(up, chip_up)
    sent = jnp.concatenate([swap, up[BLOCK:], down[BLOCK:]], axis=0)
    swap = exchange(sent, core_swap)
    ordered, count = call(
        unpack_kernel,
        [((N_CHAN * ROWS, LANES), BF16), ((128, 128), F32)],
        (sent, down, up, over, far, swap),
        scratch=[pltpu.VMEM((SLOTS, LANES), BF16)],
    )
    full = lax.all_to_all(ordered, "chan", split_axis=0, concat_axis=0, tiled=True)
    full, weights = lax.optimization_barrier((full, weights))
    others = exchange(weights, core_swap)
    (attn,) = call(
        attention_kernel,
        [((N_CHAN * LANES, QUARTER), BF16)],
        (full, ln1_gain.reshape(1, C), w_qkv),
        cost=pl.CostEstimate(flops=9_000_000_000, bytes_accessed=2_000_000, transcendentals=8_400_000),
        scratch=[
            pltpu.VMEM((ROWS, C), BF16),
            pltpu.VMEM((ROWS, LANES), BF16),
            pltpu.VMEM((ROWS, LANES), BF16),
            pltpu.VMEM((LANES, ROWS), BF16),
        ],
    )
    attn = lax.all_to_all(attn, "chan", split_axis=0, concat_axis=0, tiled=True)
    cell_sum = ((CELLS, C), BF16)
    rows, mine, for_swap, for_next = call(
        mlp_kernel,
        [((QUARTER, C), BF16), ((CELLS, C), F32), cell_sum, cell_sum],
        (attn, full, ln2_gain.reshape(1, C), cell_id.reshape(1, ROWS), weights, others),
        limit=SOME_VMEM,
    )
    from_next = exchange(for_next, next_pair)
    from_swap = exchange(for_swap, core_swap)
    (message,) = call(
        message_kernel,
        [((N_CHAN * MESSAGE, LANES), BF16)],
        (rows, mine, from_next, from_swap),
    )
    got = lax.all_to_all(message, "chan", split_axis=0, concat_axis=0, tiled=True)
    block_out, pooled = call(
        pool_kernel, [((ROWS, LANES), BF16), ((CELLS, LANES), BF16)], (got, count)
    )
    return (block_out, pooled)


def solution(mesh):
    return jax.shard_map(
        body,
        mesh=mesh,
        in_specs=(
            P("pts", "chan"),
            P("pts"),
            P("pts"),
            P(),
            P(None, None, "chan"),
            P("chan", None),
            P(),
            P(None, "chan"),
            P("chan", None),
            P(None, "chan"),
        ),
        out_specs=(P("pts", "chan"), P("pts", "chan")),
        check_vma=False,
    )
```

```python
import jax
import jax.numpy as jnp
from jax import lax
from jax.experimental import pallas as pl
from jax.experimental.pallas import tpu as pltpu
from jax.sharding import PartitionSpec as P

F32 = jnp.float32
BF16 = jnp.bfloat16

N_PTS = 128
N_CHAN = 4
ROWS = 1024
C = 512
LANES = 128
HEADS_HERE = 8
HEAD_DIM = 16
QUARTER = ROWS // N_CHAN
CELLS = ROWS // 8
CAP = 192
BLOCK = CAP + 16
KINDS = 8
SLOTS = KINDS * CAP
SHARE = 128
STEP = 512
FC1, FC2, POOL, WROWS = 128, 640, 1152, 1280
MESSAGE = QUARTER + CELLS
VMEM_LIMIT = 32 * 1024 * 1024
SOME_VMEM = 32 * 1024 * 1024
ALL_VMEM = 63 * 1024 * 1024 + 512 * 1024


def chip_up(i):
    return (i + 2 if (i >> 1) % 2 == 0 else i - 2) % N_PTS


def chip_down(i):
    return (i - 2 if (i >> 1) % 2 == 0 else i + 2) % N_PTS


def core_swap(i):
    return i ^ 1


def next_pair(i):
    return (i - 1 if i % 2 == 0 else i + 1) % N_PTS


def far_pair(i):
    return (i - 3 if i % 2 == 0 else i + 3) % N_PTS


def across(i):
    return (i + N_PTS // 2) % N_PTS


def exchange(x, partner):
    return lax.ppermute(x, "pts", [(i, partner(i)) for i in range(N_PTS)])


def offsets_of(me):
    core = lax.rem(me, 2)
    chip = lax.rem(me // 2, 2)
    up = 2 - 4 * chip
    swap = 1 - 2 * core
    return [0 * me, up, up + swap, -up, swap - up, swap, 6 * core - 3, 0 * me + 64]


def matmul(a, b):
    return jnp.dot(a, b, preferred_element_type=F32)


def matmul_nt(a, b):
    return lax.dot_general(a, b, (((1,), (1,)), ((), ())), preferred_element_type=F32)


def matmul_tn(a, b):
    return lax.dot_general(a, b, (((0,), (0,)), ((), ())), preferred_element_type=F32)


def one_hot(row, height):
    index = lax.broadcasted_iota(jnp.int32, (height, row.shape[1]), 0)
    return jnp.where(index == row, 1.0, 0.0).astype(BF16)


def gelu(x):
    return 0.5 * x * (1.0 + lax.erf(x * 0.7071067811865476))


def normed_chunks(chunks, gains):
    total = chunks[0]
    for x in chunks[1:]:
        total = total + x
    mean = jnp.sum(total, axis=-1, keepdims=True) * (1.0 / C)
    centered = [x - mean for x in chunks]
    square = centered[0] * centered[0]
    for x in centered[1:]:
        square = square + x * x
    var = jnp.sum(square, axis=-1, keepdims=True) * (1.0 / C)
    scale = lax.rsqrt(var + 1e-05)
    return [(x * scale * g).astype(BF16) for x, g in zip(centered, gains)]


def copier(sems):
    copies = []

    def start(src, dst):
        copy = pltpu.make_async_copy(src, dst, sems.at[len(copies)])
        copy.start()
        copies.append(copy)
        return copy

    return start


def wait(copies):
    for copy in copies:
        copy.wait()


def digits_of(dest):
    local = dest & (ROWS - 1)
    line = lax.broadcasted_iota(jnp.int32, (16, ROWS), 0)
    digits = jnp.where(line == 0, (local >> 5) + 1, jnp.where(line == 1, local & 31, 0))
    return digits.astype(F32).astype(BF16)


def cell_counts(cell, me):
    relative = cell - (me - 1) * CELLS
    counts = matmul_nt(jnp.full((16, ROWS), 1.0, BF16), one_hot(relative, 3 * CELLS))
    return counts[0:1, :].astype(jnp.int32)


def write_blocks(slot, dest, feats, blocks, counts):
    small = lax.broadcasted_iota(jnp.int32, (16, 128), 0)
    lane = lax.broadcasted_iota(jnp.int32, (1, 128), 1)
    chosen = one_hot(slot, SLOTS)
    packed = matmul(chosen, feats).astype(BF16)
    places = matmul_nt(digits_of(dest), chosen)
    for m, (ref, base, offset) in enumerate(blocks):
        ref[base : base + 128, :] = packed[m * 128 : (m + 1) * 128, :]
        ref[base + 128 : base + CAP, :] = packed[1024 + m * 64 : 1024 + (m + 1) * 64, :]
        first = places[0:2, m * 128 : (m + 1) * 128]
        mine = (lane >= 64) if m % 2 else (lane < 64)
        tile = 1024 + (m // 2) * 128
        second = jnp.where(mine, places[0:2, tile : tile + 128], 0.0)
        count = jnp.zeros((1, CELLS), jnp.int32)
        for away in (-1, 0, 1):
            near = jnp.where(offset == away, 1, 0)
            count = count + counts[:, (away + 1) * CELLS : (away + 2) * CELLS] * near
        rows = [
            first[0:1], first[1:2], second[0:1], second[1:2],
            (count >> 5).astype(F32), (count & 31).astype(F32),
        ]
        notes = jnp.zeros((16, 128), F32)
        for r, value in enumerate(rows):
            notes = jnp.where(small == r, value, notes)
        ref[base + CAP : base + BLOCK, :] = notes.astype(BF16)


def quarter_of(me):
    return lax.rem(me, 4)


def weights_kernel(w_out_ref, w_fc1_ref, w_fc2_ref, w_pool_ref, out_ref, sems):
    mine = quarter_of(lax.axis_index("pts"))
    start = copier(sems)
    share = pl.multiple_of(mine * SHARE, SHARE)
    few = pl.multiple_of(mine * 32, 32)
    copies = [start(w_fc1_ref.at[:, pl.ds(share, SHARE)], out_ref.at[FC1 : FC1 + C, :])]
    for r in range(4):
        cols = slice(r * 128, (r + 1) * 128)
        dst = out_ref.at[FC2 + r * SHARE : FC2 + (r + 1) * SHARE, :]
        copies.append(start(w_fc2_ref.at[pl.ds(share, SHARE), cols], dst))
        dst = out_ref.at[r * 32 : (r + 1) * 32, :]
        copies.append(start(w_out_ref.at[pl.ds(few, 32), cols], dst))
    copies.append(start(w_pool_ref.at[pl.ds(share, SHARE), :], out_ref.at[POOL:WROWS, :]))
    wait(copies)


def pack_kernel(
    feats_ref, dest_ref, cell_ref, up_ref, down_ref, swap_ref, far_ref, across_ref,
    feats_here, dest_here, cell_here, sems,
):
    me = lax.axis_index("pts")
    start = copier(sems)
    dest_copy = start(dest_ref, dest_here)
    cell_copy = start(cell_ref, cell_here)
    feats_copy = start(feats_ref, feats_here)
    before = lax.broadcasted_iota(jnp.int32, (ROWS, ROWS), 0)
    after = lax.broadcasted_iota(jnp.int32, (ROWS, ROWS), 1)
    earlier = jnp.where(before < after, 1.0, 0.0).astype(BF16)
    wait([dest_copy])
    offsets = offsets_of(me)
    dest = dest_here[...]
    away = ((dest >> 10) - me) & (N_PTS - 1)
    kind = jnp.zeros_like(dest)
    for m in range(1, KINDS):
        kind = jnp.where(away == (offsets[m] & (N_PTS - 1)), m, kind)

    kinds = one_hot(kind, 16)
    ranks = matmul(kinds, earlier) * kinds.astype(F32)
    rank = jnp.sum(ranks, axis=0, keepdims=True).astype(jnp.int32)
    slot = jnp.where(rank < 128, kind * 128 + rank, 1024 - 128 + kind * 64 + rank)
    homes = [
        (swap_ref, BLOCK), (up_ref, 0), (up_ref, BLOCK), (down_ref, 0),
        (down_ref, BLOCK), (swap_ref, 0), (far_ref, 0), (across_ref, 0),
    ]
    blocks = [home + (offset,) for home, offset in zip(homes, offsets)]
    wait([cell_copy])
    counts = cell_counts(cell_here[...], me)
    wait([feats_copy])
    write_blocks(slot, dest, feats_here[...], blocks, counts)


def unpack_kernel(sent_ref, down_ref, up_ref, across_ref, far_ref, swap_ref, out_ref, count_ref, held):
    homes = [
        (sent_ref, BLOCK), (up_ref, 0), (swap_ref, 2 * BLOCK), (down_ref, 0),
        (swap_ref, 3 * BLOCK), (swap_ref, 0), (far_ref, 0), (across_ref, 0),
    ]
    firsts, seconds = [], []
    count = jnp.zeros((1, 128), F32)
    for m, (ref, base) in enumerate(homes):
        held[m * 128 : (m + 1) * 128, :] = ref[base : base + 128, :]
        held[1024 + m * 64 : 1024 + (m + 1) * 64, :] = ref[base + 128 : base + CAP, :]
        notes = ref[base + CAP : base + BLOCK, :].astype(F32)
        firsts.append(notes[0:1] * 32.0 + notes[1:2] - 32.0)
        seconds.append(notes[2:3] * 32.0 + notes[3:4])
        count = count + notes[4:5] * 32.0 + notes[5:6]
    pairs = [seconds[m] + seconds[m + 1] - 32.0 for m in range(0, KINDS, 2)]
    places = jnp.concatenate(firsts + pairs, axis=1).astype(jnp.int32)
    ordered = matmul(one_hot(places, ROWS), held[...]).astype(BF16)
    for c in range(N_CHAN):
        out_ref[c * ROWS : (c + 1) * ROWS, :] = ordered
    count_ref[...] = jnp.broadcast_to(count, (128, 128)).T


def attention_kernel(x_ref, gain_ref, w_ref, out_ref, normed, q_ref, k_ref, v_ref):
    gains = [gain_ref[:, c * 128 : (c + 1) * 128] for c in range(4)]
    for r in range(4):
        rows = slice(r * 256, (r + 1) * 256)
        chunks = [x_ref[c * ROWS + r * 256 : c * ROWS + (r + 1) * 256, :].astype(F32) for c in range(4)]
        for c, part in enumerate(normed_chunks(chunks, gains)):
            normed[rows, c * 128 : (c + 1) * 128] = part
    everything = normed[...]
    q_ref[...] = (matmul(everything, w_ref[0]).astype(BF16).astype(F32) * 0.25).astype(BF16)
    k_ref[...] = matmul(everything, w_ref[1]).astype(BF16)
    v_ref[...] = matmul(everything, w_ref[2]).T.astype(BF16)
    head_of = lax.broadcasted_iota(jnp.int32, (STEP, LANES), 1) // HEAD_DIM
    work = [(h, part) for h in range(HEADS_HERE) for part in range(ROWS // STEP)]

    def scores_of(h, part):
        query = q_ref[part * STEP : (part + 1) * STEP, :].astype(F32)
        query = jnp.where(head_of == h, query, 0.0).astype(BF16)
        return matmul_nt(k_ref[...], query)

    scores = scores_of(*work[0])
    for n, (h, part) in enumerate(work):
        following = scores_of(*work[n + 1]) if n + 1 < len(work) else None
        top = jnp.max(scores, axis=0, keepdims=True)
        grown = jnp.exp(scores - top)
        share = 1.0 / jnp.sum(grown, axis=0, keepdims=True)
        probs = (grown * share).astype(BF16)
        result = matmul(v_ref[h * HEAD_DIM : (h + 1) * HEAD_DIM, :], probs).astype(BF16)
        for u in range(STEP // QUARTER):
            row = (part * (STEP // QUARTER) + u) * LANES + h * HEAD_DIM
            out_ref[row : row + HEAD_DIM, :] = result[:, u * QUARTER : (u + 1) * QUARTER]
        scores = following


def mlp_kernel(
    attn_ref, x_ref, gain_ref, cell_ref, mine_ref, chip_ref, core_ref, both_ref,
    block_ref, own_ref, swap_ref, next_ref,
):
    chan = lax.axis_index("chan")
    me = lax.axis_index("pts")
    core = lax.rem(me, 2)
    row = pl.multiple_of(chan * QUARTER, QUARTER)

    def columns(ref, base, height, count):
        return jnp.concatenate([ref[base + r * height : base + (r + 1) * height, :] for r in range(count)], axis=1)

    def stacked(parts):
        return jnp.concatenate(parts, axis=0)

    x = jnp.concatenate([x_ref[pl.ds(c * ROWS + row, QUARTER), :] for c in range(4)], axis=1)
    q = quarter_of(me)
    other_core = q + 1 - 2 * core
    quarters = [
        (q, mine_ref), (lax.rem(q + 2, 4), chip_ref),
        (other_core, core_ref), (lax.rem(other_core + 2, 4), both_ref),
    ]
    rows, w_out = [], []
    for which, ref in quarters:
        for c in range(4):
            rows.append(attn_ref[pl.ds(pl.multiple_of(c * 128 + which * 32, 32), 32), :])
            w_out.append(columns(ref, c * WROWS, 32, 4))
    mid = (x.astype(F32) + matmul_tn(stacked(rows), stacked(w_out))).astype(BF16).astype(F32)
    normed = normed_chunks([mid], [gain_ref[...]])[0]
    summed = None
    for _, ref in quarters:
        bases = [c * WROWS for c in range(4)]
        w_fc1 = jnp.concatenate([ref[base + FC1 : base + FC1 + C, :] for base in bases], axis=1)
        w_fc2 = stacked([columns(ref, base + FC2, SHARE, 4) for base in bases])
        act = gelu(matmul(normed, w_fc1)).astype(BF16)
        term = matmul(act, w_fc2)
        summed = term if summed is None else summed + term
    block = (mid + summed).astype(BF16)
    block_ref[...] = block
    parts, w_pool = [], []
    for which, ref in quarters:
        parts.append(block_ref[:, pl.ds(pl.multiple_of(which * 128, 128), 128)])
        w_pool.append(jnp.concatenate([ref[c * WROWS + POOL : (c + 1) * WROWS, :] for c in range(4)], axis=1))
    lin = matmul(jnp.concatenate(parts, axis=1), stacked(w_pool))
    high = lin.astype(BF16)
    low = (lin - high.astype(F32)).astype(BF16)
    member = one_hot(cell_ref[:, pl.ds(row, QUARTER)] - (me - 1) * CELLS, 3 * CELLS)
    sums = matmul(member, high) + matmul(member, low)
    own_ref[...] = sums[CELLS : 2 * CELLS]
    before = sums[:CELLS].astype(BF16)
    after = sums[2 * CELLS :].astype(BF16)

    @pl.when(core == 0)
    def _():
        swap_ref[...] = after
        next_ref[...] = before

    @pl.when(core == 1)
    def _():
        swap_ref[...] = before
        next_ref[...] = after


def message_kernel(block_ref, own_ref, next_ref, swap_ref, out_ref):
    sums = own_ref[...] + swap_ref[...].astype(F32) + next_ref[...].astype(F32)
    sums = sums.astype(BF16)
    for c in range(N_CHAN):
        cols = slice(c * 128, (c + 1) * 128)
        out_ref[c * MESSAGE : c * MESSAGE + QUARTER, :] = block_ref[:, cols]
        out_ref[c * MESSAGE + QUARTER : (c + 1) * MESSAGE, :] = sums[:, cols]


def pool_kernel(got_ref, count_ref, block_ref, out_ref):
    total = jnp.zeros((CELLS, LANES), F32)
    for c in range(N_CHAN):
        block_ref[c * QUARTER : (c + 1) * QUARTER, :] = got_ref[c * MESSAGE : c * MESSAGE + QUARTER, :]
        total = total + got_ref[c * MESSAGE + QUARTER : (c + 1) * MESSAGE, :].astype(F32)
    out_ref[...] = gelu(total / count_ref[...]).astype(BF16)


def call(kernel, outs, args, scratch=(), in_hbm=(), limit=VMEM_LIMIT, cost=None):
    vmem = pl.BlockSpec(memory_space=pltpu.VMEM)
    hbm = pl.BlockSpec(memory_space=pltpu.HBM)
    return pl.pallas_call(
        kernel,
        out_shape=[jax.ShapeDtypeStruct(shape, dtype) for shape, dtype in outs],
        in_specs=[hbm if i in in_hbm else vmem for i in range(len(args))],
        out_specs=[vmem] * len(outs),
        scratch_shapes=list(scratch),
        compiler_params=pltpu.CompilerParams(vmem_limit_bytes=limit),
        cost_estimate=cost,
    )(*args)


def body(feats, dest_pos, cell_id, ln1_gain, w_qkv, w_out, ln2_gain, w_fc1, w_fc2, w_pool):
    def block(count=1):
        return ((count * BLOCK, LANES), BF16)

    (weights,) = call(
        weights_kernel,
        [((WROWS, LANES), BF16)],
        (w_out, w_fc1, w_fc2, w_pool),
        scratch=[pltpu.SemaphoreType.DMA((10,))],
        limit=ALL_VMEM,
        in_hbm=range(4),
    )
    weights = lax.all_gather(weights, "chan", axis=0, tiled=True)
    up, down, swap, far, over = call(
        pack_kernel,
        [block(2), block(2), block(2), block(), block()],
        (feats, dest_pos.reshape(1, ROWS), cell_id.reshape(1, ROWS)),
        scratch=[
            pltpu.VMEM((ROWS, LANES), BF16),
            pltpu.VMEM((1, ROWS), jnp.int32),
            pltpu.VMEM((1, ROWS), jnp.int32),
            pltpu.SemaphoreType.DMA((3,)),
        ],
        limit=ALL_VMEM,
        in_hbm=range(3),
    )
    far = exchange(far, far_pair)
    over = exchange(over, across)
    down = exchange(down, chip_down)
    up, far, over = lax.optimization_barrier((up, far, over))
    up = exchange(up, chip_up)
    sent = jnp.concatenate([swap, up[BLOCK:], down[BLOCK:]], axis=0)
    swap = exchange(sent, core_swap)
    ordered, count = call(
        unpack_kernel,
        [((N_CHAN * ROWS, LANES), BF16), ((128, 128), F32)],
        (sent, down, up, over, far, swap),
        scratch=[pltpu.VMEM((SLOTS, LANES), BF16)],
    )
    ordered, weights = lax.optimization_barrier((ordered, weights))
    from_chip = exchange(weights, chip_up)
    full = lax.all_to_all(ordered, "chan", split_axis=0, concat_axis=0, tiled=True)
    full, weights = lax.optimization_barrier((full, weights))
    from_core = exchange(weights, core_swap)
    (attn,) = call(
        attention_kernel,
        [((N_CHAN * LANES, QUARTER), BF16)],
        (full, ln1_gain.reshape(1, C), w_qkv),
        cost=pl.CostEstimate(flops=9_000_000_000, bytes_accessed=2_000_000, transcendentals=8_400_000),
        scratch=[
            pltpu.VMEM((ROWS, C), BF16),
            pltpu.VMEM((ROWS, LANES), BF16),
            pltpu.VMEM((ROWS, LANES), BF16),
            pltpu.VMEM((LANES, ROWS), BF16),
        ],
    )
    attn, from_chip = lax.optimization_barrier((attn, from_chip))
    from_both = exchange(from_chip, core_swap)
    attn = lax.all_to_all(attn, "chan", split_axis=0, concat_axis=0, tiled=True)
    cell_sum = ((CELLS, C), BF16)
    rows, mine, for_swap, for_next = call(
        mlp_kernel,
        [((QUARTER, C), BF16), ((CELLS, C), F32), cell_sum, cell_sum],
        (attn, full, ln2_gain.reshape(1, C), cell_id.reshape(1, ROWS), weights, from_chip, from_core, from_both),
        limit=SOME_VMEM,
    )
    from_next = exchange(for_next, next_pair)
    from_swap = exchange(for_swap, core_swap)
    (message,) = call(
        message_kernel,
        [((N_CHAN * MESSAGE, LANES), BF16)],
        (rows, mine, from_next, from_swap),
    )
    got = lax.all_to_all(message, "chan", split_axis=0, concat_axis=0, tiled=True)
    block_out, pooled = call(
        pool_kernel, [((ROWS, LANES), BF16), ((CELLS, LANES), BF16)], (got, count)
    )
    return (block_out, pooled)


def solution(mesh):
    return jax.shard_map(
        body,
        mesh=mesh,
        in_specs=(
            P("pts", "chan"),
            P("pts"),
            P("pts"),
            P(),
            P(None, None, "chan"),
            P("chan", None),
            P(),
            P(None, "chan"),
            P("chan", None),
            P(None, "chan"),
        ),
        out_specs=(P("pts", "chan"), P("pts", "chan")),
        check_vma=False,
    )
```

```python
import jax
import jax.numpy as jnp
from jax import lax
from jax.experimental import pallas as pl
from jax.experimental.pallas import tpu as pltpu
from jax.sharding import PartitionSpec as P

F32 = jnp.float32
BF16 = jnp.bfloat16

N_PTS = 128
N_CHAN = 4
ROWS = 1024
C = 512
LANES = 128
HEADS_HERE = 8
HEAD_DIM = 16
QUARTER = ROWS // N_CHAN
CELLS = ROWS // 8
CAP = 192
BLOCK = CAP + 16
KINDS = 8
SLOTS = KINDS * CAP
HALF = 256
STEP = 512
FC1, FC2, POOL, WROWS = 256, 1280, 2304, 2560
MESSAGE = QUARTER + CELLS
VMEM_LIMIT = 32 * 1024 * 1024
SOME_VMEM = 32 * 1024 * 1024
ALL_VMEM = 63 * 1024 * 1024 + 512 * 1024


def chip_up(i):
    return (i + 2 if (i >> 1) % 2 == 0 else i - 2) % N_PTS


def chip_down(i):
    return (i - 2 if (i >> 1) % 2 == 0 else i + 2) % N_PTS


def core_swap(i):
    return i ^ 1


def next_pair(i):
    return (i - 1 if i % 2 == 0 else i + 1) % N_PTS


def far_pair(i):
    return (i - 3 if i % 2 == 0 else i + 3) % N_PTS


def across(i):
    return (i + N_PTS // 2) % N_PTS


def exchange(x, partner):
    return lax.ppermute(x, "pts", [(i, partner(i)) for i in range(N_PTS)])


def offsets_of(me):
    core = lax.rem(me, 2)
    chip = lax.rem(me // 2, 2)
    up = 2 - 4 * chip
    swap = 1 - 2 * core
    return [0 * me, up, up + swap, -up, swap - up, swap, 6 * core - 3, 0 * me + 64]


def matmul(a, b):
    return jnp.dot(a, b, preferred_element_type=F32)


def matmul_nt(a, b):
    return lax.dot_general(a, b, (((1,), (1,)), ((), ())), preferred_element_type=F32)


def matmul_tn(a, b):
    return lax.dot_general(a, b, (((0,), (0,)), ((), ())), preferred_element_type=F32)


def one_hot(row, height):
    index = lax.broadcasted_iota(jnp.int32, (height, row.shape[1]), 0)
    return jnp.where(index == row, 1.0, 0.0).astype(BF16)


def gelu(x):
    return 0.5 * x * (1.0 + lax.erf(x * 0.7071067811865476))


def normed_chunks(chunks, gains):
    total = chunks[0]
    for x in chunks[1:]:
        total = total + x
    mean = jnp.sum(total, axis=-1, keepdims=True) * (1.0 / C)
    centered = [x - mean for x in chunks]
    square = centered[0] * centered[0]
    for x in centered[1:]:
        square = square + x * x
    var = jnp.sum(square, axis=-1, keepdims=True) * (1.0 / C)
    scale = lax.rsqrt(var + 1e-05)
    return [(x * scale * g).astype(BF16) for x, g in zip(centered, gains)]


def copier(sems):
    copies = []

    def start(src, dst):
        copy = pltpu.make_async_copy(src, dst, sems.at[len(copies)])
        copy.start()
        copies.append(copy)
        return copy

    return start


def wait(copies):
    for copy in copies:
        copy.wait()


def digits_of(dest):
    local = dest & (ROWS - 1)
    line = lax.broadcasted_iota(jnp.int32, (16, ROWS), 0)
    digits = jnp.where(line == 0, (local >> 5) + 1, jnp.where(line == 1, local & 31, 0))
    return digits.astype(F32).astype(BF16)


def cell_counts(cell, me):
    relative = cell - (me - 1) * CELLS
    counts = matmul_nt(jnp.full((16, ROWS), 1.0, BF16), one_hot(relative, 3 * CELLS))
    return counts[0:1, :].astype(jnp.int32)


def write_blocks(slot, dest, feats, blocks, counts):
    small = lax.broadcasted_iota(jnp.int32, (16, 128), 0)
    lane = lax.broadcasted_iota(jnp.int32, (1, 128), 1)
    chosen = one_hot(slot, SLOTS)
    eye_row = lax.broadcasted_iota(jnp.int32, (16, LANES), 0)
    eye_col = lax.broadcasted_iota(jnp.int32, (16, LANES), 1)
    eye = jnp.where(eye_row == eye_col, 1.0, 0.0).astype(BF16)
    columns = matmul_tn(digits_of(dest), eye).astype(BF16)
    picked = matmul(chosen, jnp.concatenate([feats, columns], axis=1)).astype(BF16)
    packed = picked[:, :LANES]
    places = matmul_nt(eye, picked[:, LANES:])
    for m, (ref, base, offset) in enumerate(blocks):
        ref[base : base + 128, :] = packed[m * 128 : (m + 1) * 128, :]
        ref[base + 128 : base + CAP, :] = packed[1024 + m * 64 : 1024 + (m + 1) * 64, :]
        first = places[0:2, m * 128 : (m + 1) * 128]
        mine = (lane >= 64) if m % 2 else (lane < 64)
        tile = 1024 + (m // 2) * 128
        second = jnp.where(mine, places[0:2, tile : tile + 128], 0.0)
        count = jnp.zeros((1, CELLS), jnp.int32)
        for away in (-1, 0, 1):
            near = jnp.where(offset == away, 1, 0)
            count = count + counts[:, (away + 1) * CELLS : (away + 2) * CELLS] * near
        rows = [
            first[0:1], first[1:2], second[0:1], second[1:2],
            (count >> 5).astype(F32), (count & 31).astype(F32),
        ]
        notes = jnp.zeros((16, 128), F32)
        for r, value in enumerate(rows):
            notes = jnp.where(small == r, value, notes)
        ref[base + CAP : base + BLOCK, :] = notes.astype(BF16)


def weights_kernel(w_out_ref, w_fc1_ref, w_fc2_ref, w_pool_ref, out_ref, sems):
    core = lax.rem(lax.axis_index("pts"), 2)
    start = copier(sems)
    half = pl.multiple_of(core * HALF, HALF)
    quarter = pl.multiple_of(core * 64, 64)
    copies = []
    for r in range(2):
        src = w_fc1_ref.at[:, pl.ds(pl.multiple_of(half + r * 128, 128), 128)]
        copies.append(start(src, out_ref.at[FC1 + r * C : FC1 + (r + 1) * C, :]))
    for r in range(4):
        cols = slice(r * 128, (r + 1) * 128)
        dst = out_ref.at[FC2 + r * HALF : FC2 + (r + 1) * HALF, :]
        copies.append(start(w_fc2_ref.at[pl.ds(half, HALF), cols], dst))
        dst = out_ref.at[r * 64 : (r + 1) * 64, :]
        copies.append(start(w_out_ref.at[pl.ds(quarter, 64), cols], dst))
    copies.append(start(w_pool_ref.at[pl.ds(half, HALF), :], out_ref.at[POOL:WROWS, :]))
    wait(copies)


def pack_kernel(
    feats_ref, dest_ref, cell_ref, up_ref, down_ref, swap_ref, far_ref, across_ref,
    feats_here, dest_here, cell_here, sems,
):
    me = lax.axis_index("pts")
    start = copier(sems)
    dest_copy = start(dest_ref, dest_here)
    cell_copy = start(cell_ref, cell_here)
    feats_copy = start(feats_ref, feats_here)
    before = lax.broadcasted_iota(jnp.int32, (ROWS, ROWS), 0)
    after = lax.broadcasted_iota(jnp.int32, (ROWS, ROWS), 1)
    earlier = jnp.where(before < after, 1.0, 0.0).astype(BF16)
    wait([dest_copy])
    offsets = offsets_of(me)
    dest = dest_here[...]
    away = ((dest >> 10) - me) & (N_PTS - 1)
    kind = jnp.zeros_like(dest)
    for m in range(1, KINDS):
        kind = jnp.where(away == (offsets[m] & (N_PTS - 1)), m, kind)

    kinds = one_hot(kind, 16)
    ranks = matmul(kinds, earlier) * kinds.astype(F32)
    rank = jnp.sum(ranks, axis=0, keepdims=True).astype(jnp.int32)
    slot = jnp.where(rank < 128, kind * 128 + rank, 1024 - 128 + kind * 64 + rank)
    homes = [
        (swap_ref, BLOCK), (up_ref, 0), (up_ref, BLOCK), (down_ref, 0),
        (down_ref, BLOCK), (swap_ref, 0), (far_ref, 0), (across_ref, 0),
    ]
    blocks = [home + (offset,) for home, offset in zip(homes, offsets)]
    wait([cell_copy])
    counts = cell_counts(cell_here[...], me)
    wait([feats_copy])
    write_blocks(slot, dest, feats_here[...], blocks, counts)


def unpack_kernel(sent_ref, down_ref, up_ref, across_ref, far_ref, swap_ref, out_ref, count_ref, held):
    homes = [
        (sent_ref, BLOCK), (up_ref, 0), (swap_ref, 2 * BLOCK), (down_ref, 0),
        (swap_ref, 3 * BLOCK), (swap_ref, 0), (far_ref, 0), (across_ref, 0),
    ]
    firsts, seconds = [], []
    count = jnp.zeros((1, 128), F32)
    for m, (ref, base) in enumerate(homes):
        held[m * 128 : (m + 1) * 128, :] = ref[base : base + 128, :]
        held[1024 + m * 64 : 1024 + (m + 1) * 64, :] = ref[base + 128 : base + CAP, :]
        notes = ref[base + CAP : base + BLOCK, :].astype(F32)
        firsts.append(notes[0:1] * 32.0 + notes[1:2] - 32.0)
        seconds.append(notes[2:3] * 32.0 + notes[3:4])
        count = count + notes[4:5] * 32.0 + notes[5:6]
    pairs = [seconds[m] + seconds[m + 1] - 32.0 for m in range(0, KINDS, 2)]
    places = jnp.concatenate(firsts + pairs, axis=1).astype(jnp.int32)
    ordered = matmul(one_hot(places, ROWS), held[...]).astype(BF16)
    for c in range(N_CHAN):
        out_ref[c * ROWS : (c + 1) * ROWS, :] = ordered
    count_ref[...] = jnp.broadcast_to(count, (128, 128)).T


def attention_kernel(x_ref, gain_ref, w_ref, out_ref, normed, q_ref, k_ref, v_ref):
    gains = [gain_ref[:, c * 128 : (c + 1) * 128] for c in range(4)]
    for r in range(4):
        rows = slice(r * 256, (r + 1) * 256)
        chunks = [x_ref[c * ROWS + r * 256 : c * ROWS + (r + 1) * 256, :].astype(F32) for c in range(4)]
        for c, part in enumerate(normed_chunks(chunks, gains)):
            normed[rows, c * 128 : (c + 1) * 128] = part
    everything = normed[...]
    qkv = matmul(everything, jnp.concatenate([w_ref[t] for t in range(3)], axis=1))
    q_ref[...] = (qkv[:, :LANES].astype(BF16).astype(F32) * 0.25).astype(BF16)
    k_ref[...] = qkv[:, LANES : 2 * LANES].astype(BF16)
    v_ref[...] = qkv[:, 2 * LANES :].T.astype(BF16)
    head_of = lax.broadcasted_iota(jnp.int32, (STEP, LANES), 1) // HEAD_DIM
    work = [(h, part) for h in range(HEADS_HERE) for part in range(ROWS // STEP)]

    def scores_of(h, part):
        query = q_ref[part * STEP : (part + 1) * STEP, :].astype(F32)
        query = jnp.where(head_of == h, query, 0.0).astype(BF16)
        return matmul_nt(k_ref[...], query)

    scores = scores_of(*work[0])
    for n, (h, part) in enumerate(work):
        following = scores_of(*work[n + 1]) if n + 1 < len(work) else None
        top = jnp.max(scores, axis=0, keepdims=True)
        grown = jnp.exp(scores - top)
        share = 1.0 / jnp.sum(grown, axis=0, keepdims=True)
        probs = (grown * share).astype(BF16)
        result = matmul(v_ref[h * HEAD_DIM : (h + 1) * HEAD_DIM, :], probs).astype(BF16)
        for u in range(STEP // QUARTER):
            row = (part * (STEP // QUARTER) + u) * LANES + h * HEAD_DIM
            out_ref[row : row + HEAD_DIM, :] = result[:, u * QUARTER : (u + 1) * QUARTER]
        scores = following


def mlp_kernel(
    attn_ref, x_ref, gain_ref, cell_ref, mine_ref, other_ref,
    block_ref, own_ref, swap_ref, next_ref,
):
    chan = lax.axis_index("chan")
    me = lax.axis_index("pts")
    core = lax.rem(me, 2)
    row = pl.multiple_of(chan * QUARTER, QUARTER)

    def columns(ref, base, height, count):
        return jnp.concatenate([ref[base + r * height : base + (r + 1) * height, :] for r in range(count)], axis=1)

    def stacked(parts):
        return jnp.concatenate(parts, axis=0)

    x = jnp.concatenate([x_ref[pl.ds(c * ROWS + row, QUARTER), :] for c in range(4)], axis=1)
    halves = ((core, mine_ref), (1 - core, other_ref))
    rows, w_out = [], []
    for which, ref in halves:
        for c in range(4):
            rows.append(attn_ref[pl.ds(pl.multiple_of(c * 128 + which * 64, 64), 64), :])
            w_out.append(columns(ref, c * WROWS, 64, 4))
    mid = (x.astype(F32) + matmul_tn(stacked(rows), stacked(w_out))).astype(BF16).astype(F32)
    normed = normed_chunks([mid], [gain_ref[...]])[0]
    summed = None
    for _, ref in halves:
        for c in range(0, 4, 2):
            bases = (c * WROWS, (c + 1) * WROWS)
            w_fc1 = jnp.concatenate([columns(ref, base + FC1, C, 2) for base in bases], axis=1)
            w_fc2 = stacked([columns(ref, base + FC2, HALF, 4) for base in bases])
            act = gelu(matmul(normed, w_fc1)).astype(BF16)
            term = matmul(act, w_fc2)
            summed = term if summed is None else summed + term
    block = (mid + summed).astype(BF16)
    left, right = block[:, :HALF].astype(F32), block[:, HALF:].astype(F32)
    lin = None
    for which, ref in halves:
        mine = jnp.where(which == 0, left, right).astype(BF16)
        w_pool = jnp.concatenate([ref[c * WROWS + POOL : (c + 1) * WROWS, :] for c in range(4)], axis=1)
        term = matmul(mine, w_pool)
        lin = term if lin is None else lin + term
    high = lin.astype(BF16)
    low = (lin - high.astype(F32)).astype(BF16)
    member = one_hot(cell_ref[:, pl.ds(row, QUARTER)] - (me - 1) * CELLS, 3 * CELLS)
    sums = matmul(member, high) + matmul(member, low)
    block_ref[...] = block
    own_ref[...] = sums[CELLS : 2 * CELLS]
    before = sums[:CELLS].astype(BF16)
    after = sums[2 * CELLS :].astype(BF16)

    @pl.when(core == 0)
    def _():
        swap_ref[...] = after
        next_ref[...] = before

    @pl.when(core == 1)
    def _():
        swap_ref[...] = before
        next_ref[...] = after


def message_kernel(block_ref, own_ref, next_ref, swap_ref, out_ref):
    sums = own_ref[...] + swap_ref[...].astype(F32) + next_ref[...].astype(F32)
    sums = sums.astype(BF16)
    for c in range(N_CHAN):
        cols = slice(c * 128, (c + 1) * 128)
        out_ref[c * MESSAGE : c * MESSAGE + QUARTER, :] = block_ref[:, cols]
        out_ref[c * MESSAGE + QUARTER : (c + 1) * MESSAGE, :] = sums[:, cols]


def pool_kernel(got_ref, count_ref, block_ref, out_ref):
    total = jnp.zeros((CELLS, LANES), F32)
    for c in range(N_CHAN):
        block_ref[c * QUARTER : (c + 1) * QUARTER, :] = got_ref[c * MESSAGE : c * MESSAGE + QUARTER, :]
        total = total + got_ref[c * MESSAGE + QUARTER : (c + 1) * MESSAGE, :].astype(F32)
    out_ref[...] = gelu(total / count_ref[...]).astype(BF16)


def call(kernel, outs, args, scratch=(), in_hbm=(), limit=VMEM_LIMIT, cost=None):
    vmem = pl.BlockSpec(memory_space=pltpu.VMEM)
    hbm = pl.BlockSpec(memory_space=pltpu.HBM)
    return pl.pallas_call(
        kernel,
        out_shape=[jax.ShapeDtypeStruct(shape, dtype) for shape, dtype in outs],
        in_specs=[hbm if i in in_hbm else vmem for i in range(len(args))],
        out_specs=[vmem] * len(outs),
        scratch_shapes=list(scratch),
        compiler_params=pltpu.CompilerParams(vmem_limit_bytes=limit),
        cost_estimate=cost,
    )(*args)


def body(feats, dest_pos, cell_id, ln1_gain, w_qkv, w_out, ln2_gain, w_fc1, w_fc2, w_pool):
    def block(count=1):
        return ((count * BLOCK, LANES), BF16)

    up, down, swap, far, over = call(
        pack_kernel,
        [block(2), block(2), block(2), block(), block()],
        (feats, dest_pos.reshape(1, ROWS), cell_id.reshape(1, ROWS)),
        scratch=[
            pltpu.VMEM((ROWS, LANES), BF16),
            pltpu.VMEM((1, ROWS), jnp.int32),
            pltpu.VMEM((1, ROWS), jnp.int32),
            pltpu.SemaphoreType.DMA((3,)),
        ],
        limit=ALL_VMEM,
        in_hbm=range(3),
    )
    far = exchange(far, far_pair)
    over = exchange(over, across)
    down = exchange(down, chip_down)
    up, far, over = lax.optimization_barrier((up, far, over))
    up = exchange(up, chip_up)
    w_fc1, far = lax.optimization_barrier((w_fc1, far))
    (weights,) = call(
        weights_kernel,
        [((WROWS, LANES), BF16)],
        (w_out, w_fc1, w_fc2, w_pool),
        scratch=[pltpu.SemaphoreType.DMA((11,))],
        limit=ALL_VMEM,
        in_hbm=range(4),
        cost=pl.CostEstimate(flops=0, bytes_accessed=6_000_000, transcendentals=0),
    )
    weights = lax.all_gather(weights, "chan", axis=0, tiled=True)
    sent = jnp.concatenate([swap, up[BLOCK:], down[BLOCK:]], axis=0)
    swap = exchange(sent, core_swap)
    ordered, count = call(
        unpack_kernel,
        [((N_CHAN * ROWS, LANES), BF16), ((128, 128), F32)],
        (sent, down, up, over, far, swap),
        scratch=[pltpu.VMEM((SLOTS, LANES), BF16)],
    )
    full = lax.all_to_all(ordered, "chan", split_axis=0, concat_axis=0, tiled=True)
    (attn,) = call(
        attention_kernel,
        [((N_CHAN * LANES, QUARTER), BF16)],
        (full, ln1_gain.reshape(1, C), w_qkv),
        cost=pl.CostEstimate(flops=9_000_000_000, bytes_accessed=2_000_000, transcendentals=8_400_000),
        scratch=[
            pltpu.VMEM((ROWS, C), BF16),
            pltpu.VMEM((ROWS, LANES), BF16),
            pltpu.VMEM((ROWS, LANES), BF16),
            pltpu.VMEM((LANES, ROWS), BF16),
        ],
    )
    attn, weights = lax.optimization_barrier((attn, weights))
    others = exchange(weights, core_swap)
    attn = lax.all_to_all(attn, "chan", split_axis=0, concat_axis=0, tiled=True)
    cell_sum = ((CELLS, C), BF16)
    rows, mine, for_swap, for_next = call(
        mlp_kernel,
        [((QUARTER, C), BF16), ((CELLS, C), F32), cell_sum, cell_sum],
        (attn, full, ln2_gain.reshape(1, C), cell_id.reshape(1, ROWS), weights, others),
        limit=SOME_VMEM,
    )
    from_next = exchange(for_next, next_pair)
    from_swap = exchange(for_swap, core_swap)
    (message,) = call(
        message_kernel,
        [((N_CHAN * MESSAGE, LANES), BF16)],
        (rows, mine, from_next, from_swap),
    )
    got = lax.all_to_all(message, "chan", split_axis=0, concat_axis=0, tiled=True)
    block_out, pooled = call(
        pool_kernel, [((ROWS, LANES), BF16), ((CELLS, LANES), BF16)], (got, count)
    )
    return (block_out, pooled)


def solution(mesh):
    return jax.shard_map(
        body,
        mesh=mesh,
        in_specs=(
            P("pts", "chan"),
            P("pts"),
            P("pts"),
            P(),
            P(None, None, "chan"),
            P("chan", None),
            P(),
            P(None, "chan"),
            P("chan", None),
            P(None, "chan"),
        ),
        out_specs=(P("pts", "chan"), P("pts", "chan")),
        check_vma=False,
    )
```

```python
import jax
import jax.numpy as jnp
from jax import lax
from jax.experimental import pallas as pl
from jax.experimental.pallas import tpu as pltpu
from jax.sharding import PartitionSpec as P

F32 = jnp.float32
BF16 = jnp.bfloat16

N_PTS = 128
N_CHAN = 4
ROWS = 1024
C = 512
LANES = 128
HEADS_HERE = 8
HEAD_DIM = 16
QUARTER = ROWS // N_CHAN
CELLS = ROWS // 8
CAP = 192
BLOCK = CAP + 16
KINDS = 8
SLOTS = KINDS * CAP
HALF = 256
STEP = 512
FC1, FC2, POOL, WROWS = 256, 1280, 2304, 2560
MESSAGE = QUARTER + CELLS
VMEM_LIMIT = 32 * 1024 * 1024
SOME_VMEM = 32 * 1024 * 1024
ALL_VMEM = 63 * 1024 * 1024 + 512 * 1024


def chip_up(i):
    return (i + 2 if (i >> 1) % 2 == 0 else i - 2) % N_PTS


def chip_down(i):
    return (i - 2 if (i >> 1) % 2 == 0 else i + 2) % N_PTS


def core_swap(i):
    return i ^ 1


def next_pair(i):
    return (i - 1 if i % 2 == 0 else i + 1) % N_PTS


def far_pair(i):
    return (i - 3 if i % 2 == 0 else i + 3) % N_PTS


def across(i):
    return (i + N_PTS // 2) % N_PTS


def exchange(x, partner):
    return lax.ppermute(x, "pts", [(i, partner(i)) for i in range(N_PTS)])


def offsets_of(me):
    core = lax.rem(me, 2)
    chip = lax.rem(me // 2, 2)
    up = 2 - 4 * chip
    swap = 1 - 2 * core
    return [0 * me, up, up + swap, -up, swap - up, swap, 6 * core - 3, 0 * me + 64]


def matmul(a, b):
    return jnp.dot(a, b, preferred_element_type=F32)


def matmul_nt(a, b):
    return lax.dot_general(a, b, (((1,), (1,)), ((), ())), preferred_element_type=F32)


def matmul_tn(a, b):
    return lax.dot_general(a, b, (((0,), (0,)), ((), ())), preferred_element_type=F32)


def one_hot(row, height):
    index = lax.broadcasted_iota(jnp.int32, (height, row.shape[1]), 0)
    return jnp.where(index == row, 1.0, 0.0).astype(BF16)


def gelu(x):
    return 0.5 * x * (1.0 + lax.erf(x * 0.7071067811865476))


def normed_chunks(chunks, gains):
    total = chunks[0]
    for x in chunks[1:]:
        total = total + x
    mean = jnp.sum(total, axis=-1, keepdims=True) * (1.0 / C)
    centered = [x - mean for x in chunks]
    square = centered[0] * centered[0]
    for x in centered[1:]:
        square = square + x * x
    var = jnp.sum(square, axis=-1, keepdims=True) * (1.0 / C)
    scale = lax.rsqrt(var + 1e-05)
    return [(x * scale * g).astype(BF16) for x, g in zip(centered, gains)]


def copier(sems):
    copies = []

    def start(src, dst):
        copy = pltpu.make_async_copy(src, dst, sems.at[len(copies)])
        copy.start()
        copies.append(copy)
        return copy

    return start


def wait(copies):
    for copy in copies:
        copy.wait()


def digits_of(dest):
    local = dest & (ROWS - 1)
    line = lax.broadcasted_iota(jnp.int32, (16, ROWS), 0)
    digits = jnp.where(line == 0, (local >> 5) + 1, jnp.where(line == 1, local & 31, 0))
    return digits.astype(F32).astype(BF16)


def cell_counts(cell, me):
    relative = cell - (me - 1) * CELLS
    counts = matmul_nt(jnp.full((16, ROWS), 1.0, BF16), one_hot(relative, 3 * CELLS))
    return counts[0:1, :].astype(jnp.int32)


def write_blocks(slot, dest, feats, blocks, counts):
    small = lax.broadcasted_iota(jnp.int32, (16, 128), 0)
    lane = lax.broadcasted_iota(jnp.int32, (1, 128), 1)
    chosen = one_hot(slot, SLOTS)
    eye_row = lax.broadcasted_iota(jnp.int32, (16, LANES), 0)
    eye_col = lax.broadcasted_iota(jnp.int32, (16, LANES), 1)
    eye = jnp.where(eye_row == eye_col, 1.0, 0.0).astype(BF16)
    columns = matmul_tn(digits_of(dest), eye).astype(BF16)
    picked = matmul(chosen, jnp.concatenate([feats, columns], axis=1)).astype(BF16)
    packed = picked[:, :LANES]
    places = matmul_nt(eye, picked[:, LANES:])
    for m, (ref, base, offset) in enumerate(blocks):
        ref[base : base + 128, :] = packed[m * 128 : (m + 1) * 128, :]
        ref[base + 128 : base + CAP, :] = packed[1024 + m * 64 : 1024 + (m + 1) * 64, :]
        first = places[0:2, m * 128 : (m + 1) * 128]
        mine = (lane >= 64) if m % 2 else (lane < 64)
        tile = 1024 + (m // 2) * 128
        second = jnp.where(mine, places[0:2, tile : tile + 128], 0.0)
        count = jnp.zeros((1, CELLS), jnp.int32)
        for away in (-1, 0, 1):
            near = jnp.where(offset == away, 1, 0)
            count = count + counts[:, (away + 1) * CELLS : (away + 2) * CELLS] * near
        rows = [
            first[0:1], first[1:2], second[0:1], second[1:2],
            (count >> 5).astype(F32), (count & 31).astype(F32),
        ]
        notes = jnp.zeros((16, 128), F32)
        for r, value in enumerate(rows):
            notes = jnp.where(small == r, value, notes)
        ref[base + CAP : base + BLOCK, :] = notes.astype(BF16)


def weights_kernel(w_out_ref, w_fc1_ref, w_fc2_ref, w_pool_ref, out_ref, sems):
    core = lax.rem(lax.axis_index("pts"), 2)
    start = copier(sems)
    half = pl.multiple_of(core * HALF, HALF)
    quarter = pl.multiple_of(core * 64, 64)
    copies = []
    for r in range(2):
        src = w_fc1_ref.at[:, pl.ds(pl.multiple_of(half + r * 128, 128), 128)]
        copies.append(start(src, out_ref.at[FC1 + r * C : FC1 + (r + 1) * C, :]))
    for r in range(4):
        cols = slice(r * 128, (r + 1) * 128)
        dst = out_ref.at[FC2 + r * HALF : FC2 + (r + 1) * HALF, :]
        copies.append(start(w_fc2_ref.at[pl.ds(half, HALF), cols], dst))
        dst = out_ref.at[r * 64 : (r + 1) * 64, :]
        copies.append(start(w_out_ref.at[pl.ds(quarter, 64), cols], dst))
    copies.append(start(w_pool_ref.at[pl.ds(half, HALF), :], out_ref.at[POOL:WROWS, :]))
    wait(copies)


def pack_kernel(
    feats_ref, dest_ref, cell_ref, up_ref, down_ref, swap_ref, far_ref, across_ref,
    feats_here, dest_here, cell_here, sems,
):
    me = lax.axis_index("pts")
    start = copier(sems)
    dest_copy = start(dest_ref, dest_here)
    cell_copy = start(cell_ref, cell_here)
    feats_copy = start(feats_ref, feats_here)
    before = lax.broadcasted_iota(jnp.int32, (ROWS, ROWS), 0)
    after = lax.broadcasted_iota(jnp.int32, (ROWS, ROWS), 1)
    earlier = jnp.where(before < after, 1.0, 0.0).astype(BF16)
    wait([dest_copy])
    offsets = offsets_of(me)
    dest = dest_here[...]
    away = ((dest >> 10) - me) & (N_PTS - 1)
    kind = jnp.zeros_like(dest)
    for m in range(1, KINDS):
        kind = jnp.where(away == (offsets[m] & (N_PTS - 1)), m, kind)

    kinds = one_hot(kind, 16)
    ranks = matmul(kinds, earlier) * kinds.astype(F32)
    rank = jnp.sum(ranks, axis=0, keepdims=True).astype(jnp.int32)
    slot = jnp.where(rank < 128, kind * 128 + rank, 1024 - 128 + kind * 64 + rank)
    homes = [
        (swap_ref, BLOCK), (up_ref, 0), (up_ref, BLOCK), (down_ref, 0),
        (down_ref, BLOCK), (swap_ref, 0), (far_ref, 0), (across_ref, 0),
    ]
    blocks = [home + (offset,) for home, offset in zip(homes, offsets)]
    wait([cell_copy])
    counts = cell_counts(cell_here[...], me)
    wait([feats_copy])
    write_blocks(slot, dest, feats_here[...], blocks, counts)


def unpack_kernel(sent_ref, down_ref, up_ref, across_ref, far_ref, swap_ref, out_ref, count_ref, held):
    homes = [
        (sent_ref, BLOCK), (up_ref, 0), (swap_ref, 2 * BLOCK), (down_ref, 0),
        (swap_ref, 3 * BLOCK), (swap_ref, 0), (far_ref, 0), (across_ref, 0),
    ]
    firsts, seconds = [], []
    count = jnp.zeros((1, 128), F32)
    for m, (ref, base) in enumerate(homes):
        held[m * 128 : (m + 1) * 128, :] = ref[base : base + 128, :]
        held[1024 + m * 64 : 1024 + (m + 1) * 64, :] = ref[base + 128 : base + CAP, :]
        notes = ref[base + CAP : base + BLOCK, :].astype(F32)
        firsts.append(notes[0:1] * 32.0 + notes[1:2] - 32.0)
        seconds.append(notes[2:3] * 32.0 + notes[3:4])
        count = count + notes[4:5] * 32.0 + notes[5:6]
    pairs = [seconds[m] + seconds[m + 1] - 32.0 for m in range(0, KINDS, 2)]
    places = jnp.concatenate(firsts + pairs, axis=1).astype(jnp.int32)
    ordered = matmul(one_hot(places, ROWS), held[...]).astype(BF16)
    for c in range(N_CHAN):
        out_ref[c * ROWS : (c + 1) * ROWS, :] = ordered
    count_ref[...] = jnp.broadcast_to(count, (128, 128)).T


def attention_kernel(x_ref, gain_ref, w_ref, out_ref, normed, q_ref, k_ref, v_ref):
    gains = [gain_ref[:, c * 128 : (c + 1) * 128] for c in range(4)]
    for r in range(4):
        rows = slice(r * 256, (r + 1) * 256)
        chunks = [x_ref[c * ROWS + r * 256 : c * ROWS + (r + 1) * 256, :].astype(F32) for c in range(4)]
        for c, part in enumerate(normed_chunks(chunks, gains)):
            normed[rows, c * 128 : (c + 1) * 128] = part
    everything = normed[...]
    qkv = matmul(everything, jnp.concatenate([w_ref[t] for t in range(3)], axis=1))
    q_ref[...] = (qkv[:, :LANES].astype(BF16).astype(F32) * 0.25).astype(BF16)
    k_ref[...] = qkv[:, LANES : 2 * LANES].astype(BF16)
    v_ref[...] = qkv[:, 2 * LANES :].T.astype(BF16)
    head_of = lax.broadcasted_iota(jnp.int32, (STEP, LANES), 1) // HEAD_DIM
    work = [(h, part) for h in range(HEADS_HERE) for part in range(ROWS // STEP)]

    def scores_of(h, part):
        query = q_ref[part * STEP : (part + 1) * STEP, :].astype(F32)
        query = jnp.where(head_of == h, query, 0.0).astype(BF16)
        return matmul_nt(k_ref[...], query)

    scores = scores_of(*work[0])
    for n, (h, part) in enumerate(work):
        following = scores_of(*work[n + 1]) if n + 1 < len(work) else None
        top = jnp.max(scores, axis=0, keepdims=True)
        grown = jnp.exp(scores - top)
        share = 1.0 / jnp.sum(grown, axis=0, keepdims=True)
        probs = (grown * share).astype(BF16)
        result = matmul(v_ref[h * HEAD_DIM : (h + 1) * HEAD_DIM, :], probs).astype(BF16)
        for u in range(STEP // QUARTER):
            row = (part * (STEP // QUARTER) + u) * LANES + h * HEAD_DIM
            out_ref[row : row + HEAD_DIM, :] = result[:, u * QUARTER : (u + 1) * QUARTER]
        scores = following


def mlp_kernel(
    attn_ref, x_ref, gain_ref, cell_ref, mine_ref, other_ref,
    block_ref, own_ref, swap_ref, next_ref,
):
    chan = lax.axis_index("chan")
    me = lax.axis_index("pts")
    core = lax.rem(me, 2)
    row = pl.multiple_of(chan * QUARTER, QUARTER)

    def columns(ref, base, height, count):
        return jnp.concatenate([ref[base + r * height : base + (r + 1) * height, :] for r in range(count)], axis=1)

    def stacked(parts):
        return jnp.concatenate(parts, axis=0)

    x = jnp.concatenate([x_ref[pl.ds(c * ROWS + row, QUARTER), :] for c in range(4)], axis=1)
    halves = ((core, mine_ref), (1 - core, other_ref))
    rows, w_out = [], []
    for which, ref in halves:
        for c in range(4):
            rows.append(attn_ref[pl.ds(pl.multiple_of(c * 128 + which * 64, 64), 64), :])
            w_out.append(columns(ref, c * WROWS, 64, 4))
    mid = (x.astype(F32) + matmul_tn(stacked(rows), stacked(w_out))).astype(BF16).astype(F32)
    normed = normed_chunks([mid], [gain_ref[...]])[0]
    summed = None
    for _, ref in halves:
        for c in range(0, 4, 2):
            bases = (c * WROWS, (c + 1) * WROWS)
            w_fc1 = jnp.concatenate([columns(ref, base + FC1, C, 2) for base in bases], axis=1)
            w_fc2 = stacked([columns(ref, base + FC2, HALF, 4) for base in bases])
            act = gelu(matmul(normed, w_fc1)).astype(BF16)
            term = matmul(act, w_fc2)
            summed = term if summed is None else summed + term
    block = (mid + summed).astype(BF16)
    left, right = block[:, :HALF].astype(F32), block[:, HALF:].astype(F32)
    lin = None
    for which, ref in halves:
        mine = jnp.where(which == 0, left, right).astype(BF16)
        w_pool = jnp.concatenate([ref[c * WROWS + POOL : (c + 1) * WROWS, :] for c in range(4)], axis=1)
        term = matmul(mine, w_pool)
        lin = term if lin is None else lin + term
    high = lin.astype(BF16)
    low = (lin - high.astype(F32)).astype(BF16)
    member = one_hot(cell_ref[:, pl.ds(row, QUARTER)] - (me - 1) * CELLS, 3 * CELLS)
    sums = matmul(member, high) + matmul(member, low)
    block_ref[...] = block
    own_ref[...] = sums[CELLS : 2 * CELLS]
    before = sums[:CELLS].astype(BF16)
    after = sums[2 * CELLS :].astype(BF16)

    @pl.when(core == 0)
    def _():
        swap_ref[...] = after
        next_ref[...] = before

    @pl.when(core == 1)
    def _():
        swap_ref[...] = before
        next_ref[...] = after


def message_kernel(block_ref, own_ref, next_ref, swap_ref, out_ref):
    sums = own_ref[...] + swap_ref[...].astype(F32) + next_ref[...].astype(F32)
    sums = sums.astype(BF16)
    for c in range(N_CHAN):
        cols = slice(c * 128, (c + 1) * 128)
        out_ref[c * MESSAGE : c * MESSAGE + QUARTER, :] = block_ref[:, cols]
        out_ref[c * MESSAGE + QUARTER : (c + 1) * MESSAGE, :] = sums[:, cols]


def pool_kernel(got_ref, count_ref, block_ref, out_ref):
    total = jnp.zeros((CELLS, LANES), F32)
    for c in range(N_CHAN):
        block_ref[c * QUARTER : (c + 1) * QUARTER, :] = got_ref[c * MESSAGE : c * MESSAGE + QUARTER, :]
        total = total + got_ref[c * MESSAGE + QUARTER : (c + 1) * MESSAGE, :].astype(F32)
    out_ref[...] = gelu(total / count_ref[...]).astype(BF16)


def call(kernel, outs, args, scratch=(), in_hbm=(), limit=VMEM_LIMIT, cost=None):
    vmem = pl.BlockSpec(memory_space=pltpu.VMEM)
    hbm = pl.BlockSpec(memory_space=pltpu.HBM)
    return pl.pallas_call(
        kernel,
        out_shape=[jax.ShapeDtypeStruct(shape, dtype) for shape, dtype in outs],
        in_specs=[hbm if i in in_hbm else vmem for i in range(len(args))],
        out_specs=[vmem] * len(outs),
        scratch_shapes=list(scratch),
        compiler_params=pltpu.CompilerParams(vmem_limit_bytes=limit),
        cost_estimate=cost,
    )(*args)


def body(feats, dest_pos, cell_id, ln1_gain, w_qkv, w_out, ln2_gain, w_fc1, w_fc2, w_pool):
    def block(count=1):
        return ((count * BLOCK, LANES), BF16)

    (weights,) = call(
        weights_kernel,
        [((WROWS, LANES), BF16)],
        (w_out, w_fc1, w_fc2, w_pool),
        scratch=[pltpu.SemaphoreType.DMA((11,))],
        limit=ALL_VMEM,
        in_hbm=range(4),
    )
    weights = lax.all_gather(weights, "chan", axis=0, tiled=True)
    up, down, swap, far, over = call(
        pack_kernel,
        [block(2), block(2), block(2), block(), block()],
        (feats, dest_pos.reshape(1, ROWS), cell_id.reshape(1, ROWS)),
        scratch=[
            pltpu.VMEM((ROWS, LANES), BF16),
            pltpu.VMEM((1, ROWS), jnp.int32),
            pltpu.VMEM((1, ROWS), jnp.int32),
            pltpu.SemaphoreType.DMA((3,)),
        ],
        limit=ALL_VMEM,
        in_hbm=range(3),
    )
    far = exchange(far, far_pair)
    over = exchange(over, across)
    down = exchange(down, chip_down)
    up, far, over = lax.optimization_barrier((up, far, over))
    up = exchange(up, chip_up)
    sent = jnp.concatenate([swap, up[BLOCK:], down[BLOCK:]], axis=0)
    swap = exchange(sent, core_swap)
    ordered, count = call(
        unpack_kernel,
        [((N_CHAN * ROWS, LANES), BF16), ((128, 128), F32)],
        (sent, down, up, over, far, swap),
        scratch=[pltpu.VMEM((SLOTS, LANES), BF16)],
    )
    full = lax.all_to_all(ordered, "chan", split_axis=0, concat_axis=0, tiled=True)
    full, weights = lax.optimization_barrier((full, weights))
    others = exchange(weights, core_swap)
    (attn,) = call(
        attention_kernel,
        [((N_CHAN * LANES, QUARTER), BF16)],
        (full, ln1_gain.reshape(1, C), w_qkv),
        cost=pl.CostEstimate(flops=9_000_000_000, bytes_accessed=2_000_000, transcendentals=8_400_000),
        scratch=[
            pltpu.VMEM((ROWS, C), BF16),
            pltpu.VMEM((ROWS, LANES), BF16),
            pltpu.VMEM((ROWS, LANES), BF16),
            pltpu.VMEM((LANES, ROWS), BF16),
        ],
    )
    attn = lax.all_to_all(attn, "chan", split_axis=0, concat_axis=0, tiled=True)
    cell_sum = ((CELLS, C), BF16)
    rows, mine, for_swap, for_next = call(
        mlp_kernel,
        [((QUARTER, C), BF16), ((CELLS, C), F32), cell_sum, cell_sum],
        (attn, full, ln2_gain.reshape(1, C), cell_id.reshape(1, ROWS), weights, others),
        limit=SOME_VMEM,
    )
    from_next = exchange(for_next, next_pair)
    from_swap = exchange(for_swap, core_swap)
    (message,) = call(
        message_kernel,
        [((N_CHAN * MESSAGE, LANES), BF16)],
        (rows, mine, from_next, from_swap),
    )
    got = lax.all_to_all(message, "chan", split_axis=0, concat_axis=0, tiled=True)
    block_out, pooled = call(
        pool_kernel, [((ROWS, LANES), BF16), ((CELLS, LANES), BF16)], (got, count)
    )
    return (block_out, pooled)


def solution(mesh):
    return jax.shard_map(
        body,
        mesh=mesh,
        in_specs=(
            P("pts", "chan"),
            P("pts"),
            P("pts"),
            P(),
            P(None, None, "chan"),
            P("chan", None),
            P(),
            P(None, "chan"),
            P("chan", None),
            P(None, "chan"),
        ),
        out_specs=(P("pts", "chan"), P("pts", "chan")),
        check_vma=False,
    )
```
